512 devices in a mesh: space: 32 (over x, z_hi, core), sect: 16 (over z_lo, y).
Axes of the slice: x: 4, y: 8, z: 8 (z_hi: 4, z_lo: 2; z = z_hi * 2 + z_lo), core: 2. Of those that a mesh axis runs over, the one named last changes fastest.
Arguments:
- density: float32 [96, 128, 2048], P('space', 'sect'), may hold values from 0.05 to 1
- velocity: float32 [96, 2048], P('space'), may hold values from -0.9 to 0.9
- kernel: float32 [128, 128], replicated, may hold values from 0.00078125 to 0.0078125
- split: float32 [128, 128], replicated, may hold values from 0 to 1
- target: int32 [128, 128], replicated, may hold values from 0 to 126, as said below
Outputs:
- updated: float32 [96, 128, 2048], P('space', 'sect')
The draws below stay inside these ranges and needn't reach their ends.
Inputs may be any that keep to these rules, and one draw needn't show every extreme that they name: target is symmetric, and target[i][j] is at least min(max(i, j), 126).
All inputs are finite; a program needn't handle non-finite values.
Results may differ from the reference program's by a relative error of at most 0.00058.
Values may be sent and summed in bfloat16 or wider, within the bound.
No kernel may reach another device: no remote copies, remote signals or barrier semaphores. Data moves between devices by JAX's collectives and lax.ppermute only.
A program may use at most 64 MiB of HBM per device.

```python
import math
import jax
import jax.numpy as jnp
from jax import lax

K = 128
STEPS = 4
PL = 2048
NX = 96


def draw_target(key, part):
    rows = lax.broadcasted_iota(jnp.int32, (K, K), 0)
    cols = lax.broadcasted_iota(jnp.int32, (K, K), 1)
    lowest = jnp.minimum(jnp.maximum(rows, cols), K - 2)
    spread = K - 1 - lowest
    raw = jax.random.randint(key, (K, K), 0, 1048576)
    raw = jnp.where(rows <= cols, raw, raw.T)
    return (lowest + raw % spread).astype(jnp.int32)


def block_levels(stream_key, extent, cuts, low, high):
    factor_of, own = 1.0, jax.random.fold_in(stream_key, 6)
    for position, shards_of in cuts:
        heights = jnp.exp(jax.random.uniform(jax.random.fold_in(own, position), (shards_of,), jnp.float32, low / len(cuts), high / len(cuts)))
        factor_of = factor_of * jnp.repeat(heights, extent[position] // shards_of).reshape([-1 if axis == position else 1 for axis in range(len(extent))])
    return factor_of


def setup_inputs(seed: int = 0) -> dict:
    streams_of = jax.random.split(jax.random.key(seed), 6)
    density = jnp.clip(jnp.exp(math.log(1.0) - 2.9957323 * jax.random.uniform(streams_of[0], (NX, K, PL), jnp.float32) ** block_levels(streams_of[0], (NX, K, PL), ((0, 32), (1, 16)), -0.2, 0.2)), 0.05, 1.0)
    velocity = jnp.clip(jax.random.uniform(streams_of[1], (NX, PL), jnp.float32, -0.9, 0.9) * block_levels(streams_of[1], (NX, PL), ((0, 32),), -0.4, 0.0), -0.9, 0.9)
    kernel = jnp.clip(jnp.exp(jax.random.uniform(streams_of[2], (K, K), jnp.float32, math.log(0.00078125), math.log(0.0078125))), 0.00078125, 0.0078125)
    split = jnp.clip(jax.random.uniform(streams_of[3], (K, K), jnp.float32, 0.0, 1.0), 0.0, 1.0)
    target = draw_target(jax.random.fold_in(streams_of[5], 71), 0)
    return {"density": density, "velocity": velocity, "kernel": kernel, "split": split, "target": target}


def reference(density, velocity, kernel, split, target):
    beta = 0.5 * (kernel + kernel.T)
    weight = 0.5 * (split + split.T)
    beta_low = beta.astype(jnp.bfloat16)
    ks = jnp.arange(K, dtype=jnp.int32)[:, None, None]
    tt = target[None, :, :]
    coef = (0.5 * beta[None] * (weight[None] * (ks == tt).astype(jnp.float32) + (1.0 - weight[None]) * (ks == tt + 1).astype(jnp.float32))).astype(jnp.bfloat16).reshape(K, K * K)
    coef_wide = coef.astype(jnp.float32)

    def plane(row):
        wide = row.astype(jnp.float32)
        pair = (wide[:, None, :] * wide[None, :, :]).astype(jnp.bfloat16).reshape(K * K, row.shape[-1])
        gain = jnp.dot(coef_wide, pair.astype(jnp.float32), precision=lax.Precision.HIGHEST)
        rate = jnp.dot(beta_low, row, preferred_element_type=jnp.float32)
        return gain, rate

    speed = velocity[:, None, :]
    state = density
    for step in range(STEPS):
        low = state.astype(jnp.bfloat16)
        gain, rate = lax.map(plane, low)
        ahead = jnp.roll(state, -1, axis=0)
        flux = jnp.maximum(speed, 0.0) * state + jnp.minimum(speed, 0.0) * ahead
        behind = jnp.roll(flux, 1, axis=0)
        state = state - (flux - behind) + (gain - state * rate)
    return state
```

```python
import jax
import jax.numpy as jnp
from jax import lax
from jax.experimental import pallas as pl
from jax.experimental.pallas import tpu as pltpu
from jax.sharding import Mesh
from jax.sharding import PartitionSpec as P

K = 128
CELLS = 128
BLOCKS = 8
B = 16
SECT = ("zl", "y")
SPACE = ("chip", "core")
VMEM = pl.BlockSpec(memory_space=pltpu.VMEM)
SMEM = pl.BlockSpec(memory_space=pltpu.SMEM)
F32 = jnp.float32
BF16 = jnp.bfloat16


def params(mib):
    return pltpu.CompilerParams(vmem_limit_bytes=mib * 1024 * 1024)


def prepare_kernel(kernel_ref, split_ref, target_ref, beta_ref, *coef_refs):
    kernel, split = kernel_ref[...], split_ref[...]
    beta = 0.5 * (kernel + kernel.T)
    weight = 0.5 * (split + split.T)
    beta_ref[...] = beta.astype(BF16)
    rows = lax.broadcasted_iota(jnp.int32, (K, K), 0)
    cols = lax.broadcasted_iota(jnp.int32, (K, K), 1)
    count = jnp.where(cols < rows, 2.0, jnp.where(cols == rows, 1.0, 0.0))
    low = 0.5 * beta * weight * count
    high = 0.5 * beta * (1.0 - weight) * count
    target = jnp.where(cols <= rows, target_ref[...], 0)
    for block in range(BLOCKS):
        n = B * (block + 1)
        tiles = n * B // K
        parts = [[None] * tiles for _ in range(3)]
        for jj in range(B):
            j = B * block + jj
            for which, array in enumerate((low, high, target)):
                row = array[j : j + 1]
                offset = jj * n
                first, shift = offset // K, offset % K
                if shift:
                    row = pltpu.roll(row, shift, 1)
                lane = cols[:1]
                pieces = [(first, row)]
                if shift + n > K:
                    zero = jnp.zeros_like(row)
                    pieces = [(first, jnp.where(lane >= shift, row, zero)), (first + 1, jnp.where(lane < shift, row, zero))]
                for tile, piece in pieces:
                    had = parts[which][tile]
                    parts[which][tile] = piece if had is None else had + piece
        top = K - B * block
        ks = lax.broadcasted_iota(jnp.int32, (top, K), 0) + B * block
        for tile in range(tiles):
            a, b, t = (parts[which][tile] for which in range(3))
            value = jnp.where(ks == t, a, jnp.where(ks == t + 1, b, 0.0))
            coef_refs[block][:, tile * K : (tile + 1) * K] = value.astype(BF16)


def prepare(kernel, split, target):
    shapes = [jax.ShapeDtypeStruct((K, K), BF16)]
    shapes += [jax.ShapeDtypeStruct((K - B * b, B * B * (b + 1)), BF16) for b in range(BLOCKS)]
    return pl.pallas_call(
        prepare_kernel,
        out_shape=shapes,
        in_specs=[VMEM] * 3,
        out_specs=[VMEM] * (BLOCKS + 1),
        compiler_params=params(16),
        name="prepare",
    )(kernel, split, target)


def reaction(planes, beta, coefs, pair_ref):
    x = jnp.concatenate(planes, axis=1) if len(planes) > 1 else planes[0]
    width = x.shape[1]
    low = x.astype(BF16)
    total = None
    for block in range(BLOCKS):
        n = B * (block + 1)
        for jj in range(B):
            j = B * block + jj
            factor = jnp.broadcast_to(x[j : j + 1], (B, width)).astype(BF16)
            for part in range(block + 1):
                at = jj * n + B * part
                pair_ref[at : at + B, :width] = low[B * part : B * (part + 1)] * factor
        gain = jnp.dot(coefs[block][...], pair_ref[: B * n, :width], preferred_element_type=F32)
        if block == 0:
            total = gain
        else:
            total = jnp.concatenate([total[: B * block], total[B * block :] + gain], axis=0)
    rate = jnp.dot(beta[...], low, preferred_element_type=F32)
    change = total - x * rate
    return [change[:, CELLS * p : CELLS * (p + 1)] for p in range(len(planes))]


def moved(before, here, after, speed_before, speed_here):
    out = jnp.maximum(speed_here, 0.0) * here + jnp.minimum(speed_here, 0.0) * after
    came = jnp.maximum(speed_before, 0.0) * before + jnp.minimum(speed_before, 0.0) * here
    return here - (out - came)


def unpack_kernel(core_ref, blocks_ref, speed_ref, state_ref, to_x_ref, to_s_ref):
    core = core_ref[0]
    for p in range(3):
        for d in range(16):
            state_ref[p, 8 * d : 8 * d + 8] = blocks_ref[d, p]
    for h in range(2):
        to_x_ref[h, :K] = state_ref[core + h]
        to_s_ref[h, :K] = state_ref[1 - core + h]
        to_x_ref[h, K:] = jnp.broadcast_to(speed_ref[pl.ds(core + h, 1)], (8, CELLS))
        to_s_ref[h, K:] = jnp.broadcast_to(speed_ref[pl.ds(1 - core + h, 1)], (8, CELLS))


def react_kernel(state_ref, beta_ref, *refs):
    coefs, change_ref, pair_ref = refs[:BLOCKS], refs[BLOCKS], refs[BLOCKS + 1]
    for p, change in enumerate(reaction([state_ref[p] for p in range(3)], beta_ref, coefs, pair_ref)):
        change_ref[p] = change


def react(state, beta, coefs):
    return pl.pallas_call(
        react_kernel,
        out_shape=jax.ShapeDtypeStruct((3, K, CELLS), F32),
        in_specs=[VMEM] * (2 + BLOCKS),
        out_specs=VMEM,
        scratch_shapes=[pltpu.VMEM((2048, 3 * CELLS), BF16)],
        compiler_params=params(24),
        cost_estimate=pl.CostEstimate(flops=2 * K * 9216 * 384, bytes_accessed=3000000, transcendentals=0),
        name="react",
    )(state, beta, *coefs)


def two_steps(core_ref, state_ref, change_ref, from_x_ref, from_s_ref, faces, beta_ref, coefs, pair_ref, all_ref):
    core = core_ref[0]
    for h in range(2):
        all_ref[5 * core + h] = from_x_ref[h, :K]
        all_ref[5 * (1 - core) + h] = from_s_ref[h, :K]
    first, last = reaction([all_ref[1], all_ref[5]], beta_ref, coefs, pair_ref)
    before, after = all_ref[0], all_ref[6]
    planes = [before, all_ref[1], *(state_ref[p] for p in range(3)), all_ref[5], after]
    changes = [None, first, *(change_ref[p] for p in range(3)), last]
    once = [moved(planes[p - 1], planes[p], planes[p + 1], faces[p - 1], faces[p]) + changes[p] for p in range(1, 6)]
    again = reaction(once[1:4], beta_ref, coefs, pair_ref)
    return [moved(once[q], once[q + 1], once[q + 2], faces[q + 1], faces[q + 2]) + again[q] for q in range(3)]


def first_kernel(core_ref, state_ref, change_ref, from_x_ref, from_s_ref, speed_ref, beta_ref, *refs):
    coefs = refs[:BLOCKS]
    out_ref, to_x_ref, to_s_ref, faces_ref, pair_ref, all_ref = refs[BLOCKS:]
    core = core_ref[0]
    for h in range(2):
        faces_ref[pl.ds(5 * core + h, 1)] = from_x_ref[h, K : K + 1]
        faces_ref[pl.ds(5 * (1 - core) + h, 1)] = from_s_ref[h, K : K + 1]
    faces_ref[2:5] = speed_ref[...]
    faces = [faces_ref[f : f + 1] for f in range(7)]
    states = two_steps(core_ref, state_ref, change_ref, from_x_ref, from_s_ref, faces, beta_ref, coefs, pair_ref, all_ref)
    for p in range(3):
        out_ref[p] = states[p]
    for h in range(2):
        to_x_ref[h] = out_ref[core + h]
        to_s_ref[h] = out_ref[1 - core + h]


def second_kernel(core_ref, state_ref, change_ref, from_x_ref, from_s_ref, faces_ref, beta_ref, *refs):
    coefs = refs[:BLOCKS]
    out_ref, pair_ref, all_ref = refs[BLOCKS:]
    faces = [faces_ref[f : f + 1] for f in range(7)]
    states = two_steps(core_ref, state_ref, change_ref, from_x_ref, from_s_ref, faces, beta_ref, coefs, pair_ref, all_ref)
    for p in range(3):
        for d in range(16):
            out_ref[d, p] = states[p][8 * d : 8 * d + 8]


def swap(array, odd):
    pairs = [(s, (s + 1) % 32) for s in range(32) if s % 2 == odd]
    return lax.ppermute(array, SPACE, pairs + [(b, a) for a, b in pairs])


def on_device(density, velocity, kernel, split, target):
    core = lax.axis_index("core").astype(jnp.int32).reshape(1)
    beta, *coefs = prepare(kernel, split, target)
    blocks = density.reshape(3, 8, 16, CELLS).transpose(2, 0, 1, 3)
    blocks = lax.all_to_all(blocks, SECT, split_axis=0, concat_axis=0, tiled=True)
    speed = lax.dynamic_slice_in_dim(velocity, lax.axis_index(SECT) * CELLS, CELLS, 1)
    plane, halo = jax.ShapeDtypeStruct((3, K, CELLS), F32), jax.ShapeDtypeStruct((2, K, CELLS), F32)
    wide = jax.ShapeDtypeStruct((2, K + 8, CELLS), F32)
    state, to_x, to_s = pl.pallas_call(
        unpack_kernel,
        out_shape=[plane, wide, wide],
        in_specs=[SMEM, VMEM, VMEM],
        out_specs=[VMEM] * 3,
        compiler_params=params(8),
        name="unpack",
    )(core, blocks, speed)
    scratch = [pltpu.VMEM((2048, 3 * CELLS), BF16), pltpu.VMEM((7, K, CELLS), F32)]

    from_x, from_s = swap(to_x, 1), swap(to_s, 0)
    change = react(state, beta, coefs)
    state, to_x, to_s, faces = pl.pallas_call(
        first_kernel,
        out_shape=[plane, halo, halo, jax.ShapeDtypeStruct((7, CELLS), F32)],
        in_specs=[SMEM] + [VMEM] * (6 + BLOCKS),
        out_specs=[VMEM] * 4,
        scratch_shapes=scratch,
        compiler_params=params(24),
        name="first_two",
    )(core, state, change, from_x, from_s, speed, beta, *coefs)

    from_x, from_s = swap(to_x, 1), swap(to_s, 0)
    change = react(state, beta, coefs)
    blocks = pl.pallas_call(
        second_kernel,
        out_shape=jax.ShapeDtypeStruct((16, 3, 8, CELLS), F32),
        in_specs=[SMEM] + [VMEM] * (6 + BLOCKS),
        out_specs=VMEM,
        scratch_shapes=scratch,
        compiler_params=params(24),
        name="last_two",
    )(core, state, change, from_x, from_s, faces, beta, *coefs)
    blocks = lax.all_to_all(blocks, SECT, split_axis=0, concat_axis=0, tiled=True)
    return blocks.transpose(1, 2, 0, 3).reshape(density.shape)


def solution(mesh):
    torus = Mesh(mesh.devices.reshape(16, 2, 2, 8), ("chip", "core", "zl", "y"))
    return jax.shard_map(
        on_device,
        mesh=torus,
        in_specs=(P(SPACE, SECT, None), P(SPACE, None), P(), P(), P()),
        out_specs=P(SPACE, SECT, None),
        check_vma=False,
    )
```

```python
import jax
import jax.numpy as jnp
from jax import lax
from jax.experimental import pallas as pl
from jax.experimental.pallas import tpu as pltpu
from jax.sharding import Mesh
from jax.sharding import PartitionSpec as P

K = 128
CELLS = 128
BLOCKS = 8
B = 16
SECT = ("zl", "y")
SPACE = ("chip", "core")
STEPS = 4
VMEM = pl.BlockSpec(memory_space=pltpu.VMEM)
SMEM = pl.BlockSpec(memory_space=pltpu.SMEM)
F16 = jnp.float16
F32 = jnp.float32
BF16 = jnp.bfloat16


def params(mib):
    return pltpu.CompilerParams(vmem_limit_bytes=mib * 1024 * 1024)


def prepare_kernel(kernel_ref, split_ref, target_ref, beta_ref, *coef_refs):
    kernel, split = kernel_ref[...], split_ref[...]
    beta = 0.5 * (kernel + kernel.T)
    weight = 0.5 * (split + split.T)
    beta_ref[...] = beta.astype(BF16)
    rows = lax.broadcasted_iota(jnp.int32, (K, K), 0)
    cols = lax.broadcasted_iota(jnp.int32, (K, K), 1)
    count = jnp.where(cols < rows, 2.0, jnp.where(cols == rows, 1.0, 0.0))
    low = 0.5 * beta * weight * count
    high = 0.5 * beta * (1.0 - weight) * count
    target = jnp.where(cols <= rows, target_ref[...], 0)
    for block in range(BLOCKS):
        n = B * (block + 1)
        tiles = n * B // K
        parts = [[None] * tiles for _ in range(3)]
        for jj in range(B):
            j = B * block + jj
            for which, array in enumerate((low, high, target)):
                row = array[j : j + 1]
                offset = jj * n
                first, shift = offset // K, offset % K
                if shift:
                    row = pltpu.roll(row, shift, 1)
                lane = cols[:1]
                pieces = [(first, row)]
                if shift + n > K:
                    zero = jnp.zeros_like(row)
                    pieces = [(first, jnp.where(lane >= shift, row, zero)), (first + 1, jnp.where(lane < shift, row, zero))]
                for tile, piece in pieces:
                    had = parts[which][tile]
                    parts[which][tile] = piece if had is None else had + piece
        top = K - B * block
        ks = lax.broadcasted_iota(jnp.int32, (top, K), 0) + B * block
        for tile in range(tiles):
            a, b, t = (parts[which][tile] for which in range(3))
            value = jnp.where(ks == t, a, jnp.where(ks == t + 1, b, 0.0))
            coef_refs[block][:, tile * K : (tile + 1) * K] = value.astype(BF16)


def prepare(kernel, split, target):
    shapes = [jax.ShapeDtypeStruct((K, K), BF16)]
    shapes += [jax.ShapeDtypeStruct((K - B * b, B * B * (b + 1)), BF16) for b in range(BLOCKS)]
    return pl.pallas_call(
        prepare_kernel,
        out_shape=shapes,
        in_specs=[VMEM] * 3,
        out_specs=[VMEM] * (BLOCKS + 1),
        compiler_params=params(16),
        name="prepare",
    )(kernel, split, target)


def reaction(planes, beta, coefs, pair_ref):
    x = jnp.concatenate(planes, axis=1) if len(planes) > 1 else planes[0]
    width = x.shape[1]
    low = x.astype(BF16)
    total = None
    for block in range(BLOCKS):
        n = B * (block + 1)
        for jj in range(B):
            j = B * block + jj
            factor = jnp.broadcast_to(x[j : j + 1], (B, width)).astype(BF16)
            for part in range(block + 1):
                at = jj * n + B * part
                pair_ref[at : at + B, :width] = low[B * part : B * (part + 1)] * factor
        gain = jnp.dot(coefs[block][...], pair_ref[: B * n, :width], preferred_element_type=F32)
        if block == 0:
            total = gain
        else:
            total = jnp.concatenate([total[: B * block], total[B * block :] + gain], axis=0)
    rate = jnp.dot(beta[...], low, preferred_element_type=F32)
    change = total - x * rate
    return [change[:, CELLS * p : CELLS * (p + 1)] for p in range(len(planes))]


def moved(before, here, after, speed_before, speed_here):
    out = jnp.maximum(speed_here, 0.0) * here + jnp.minimum(speed_here, 0.0) * after
    came = jnp.maximum(speed_before, 0.0) * before + jnp.minimum(speed_before, 0.0) * here
    return here - (out - came)


def steps_kernel(core_ref, chip_ref, far_ref, near_ref, beta_ref, *refs):
    coefs, out_ref, pair_ref, window_ref = refs[:BLOCKS], refs[BLOCKS], refs[BLOCKS + 1], refs[BLOCKS + 2]
    core = core_ref[0]
    for p in range(4):
        window_ref[7 * core + p] = far_ref[p]
    for p in range(6):
        window_ref[4 - 3 * core + p] = chip_ref[p]
    window_ref[10 * (1 - core)] = near_ref[...]
    planes = [window_ref[w, :K] for w in range(11)]
    faces = [window_ref[w, K : K + 1] + window_ref[w, K + 1 : K + 2] * (1.0 / 2048.0) for w in range(11)]
    for step in range(STEPS):
        inner = range(1, len(planes) - 1)
        changes = reaction([planes[w] for w in inner], beta_ref, coefs, pair_ref)
        planes = [
            moved(planes[w - 1], planes[w], planes[w + 1], faces[w - 1 + step], faces[w + step]) + changes[w - 1]
            for w in inner
        ]
    for p in range(3):
        for d in range(16):
            out_ref[d, p] = planes[p][8 * d : 8 * d + 8] * (1.0 / 512.0)


def on_device(density, velocity, kernel, split, target):
    core = lax.axis_index("core").astype(jnp.int32)
    beta, *coefs = prepare(kernel, split, target)
    blocks = density.reshape(3, 8, 16, CELLS).transpose(2, 0, 1, 3).astype(F16)
    blocks = lax.all_to_all(blocks, SECT, split_axis=0, concat_axis=0, tiled=True)
    speed = lax.dynamic_slice_in_dim(velocity, lax.axis_index(SECT) * CELLS, CELLS, 1)
    high = speed.astype(F16)
    rest = ((speed - high.astype(F32)) * 2048.0).astype(F16)
    own = blocks.transpose(1, 0, 2, 3).reshape(3, K, CELLS)
    own = jnp.concatenate([own, high[:, None], rest[:, None], jnp.zeros((3, 14, CELLS), F16)], axis=1)
    chip = lax.all_gather(own, "core", axis=0, tiled=True)
    edge = lax.dynamic_slice_in_dim(chip, 2 * core, 4, 0)
    neighbours = [[s, (s + 1) % 32] for s in range(1, 32, 2)]
    far = lax.all_gather(edge, SPACE, axis=0, axis_index_groups=neighbours)
    far = lax.dynamic_index_in_dim(far, core, 0, keepdims=False)
    near = lax.all_gather(lax.dynamic_index_in_dim(far, 3 * (1 - core), 0, keepdims=False), "core", axis=0)
    near = lax.dynamic_index_in_dim(near, 1 - core, 0, keepdims=False)
    blocks = pl.pallas_call(
        steps_kernel,
        out_shape=jax.ShapeDtypeStruct((16, 3, 8, CELLS), F32),
        in_specs=[SMEM] + [VMEM] * (4 + BLOCKS),
        out_specs=VMEM,
        scratch_shapes=[pltpu.VMEM((2048, 9 * CELLS), BF16), pltpu.VMEM((11, K + 16, CELLS), F32)],
        compiler_params=params(32),
        name="steps",
    )(core.reshape(1), chip.astype(F32), far.astype(F32), near.astype(F32), beta, *coefs)
    blocks = lax.all_to_all(blocks.astype(F16), SECT, split_axis=0, concat_axis=0, tiled=True)
    return blocks.transpose(1, 2, 0, 3).reshape(density.shape).astype(F32) * 512.0


def solution(mesh):
    torus = Mesh(mesh.devices.reshape(16, 2, 2, 8), ("chip", "core", "zl", "y"))
    return jax.shard_map(
        on_device,
        mesh=torus,
        in_specs=(P(SPACE, SECT, None), P(SPACE, None), P(), P(), P()),
        out_specs=P(SPACE, SECT, None),
        check_vma=False,
    )
```

```python
import jax
import jax.numpy as jnp
from jax import lax
from jax.experimental import pallas as pl
from jax.experimental.pallas import tpu as pltpu
from jax.sharding import Mesh
from jax.sharding import PartitionSpec as P

K = 128
CELLS = 128
BLOCKS = 8
B = 16
SECT = ("zl", "y")
SPACE = ("chip", "core")
STEPS = 4
VMEM = pl.BlockSpec(memory_space=pltpu.VMEM)
SMEM = pl.BlockSpec(memory_space=pltpu.SMEM)
F16 = jnp.float16
F32 = jnp.float32
BF16 = jnp.bfloat16


def params(mib):
    return pltpu.CompilerParams(vmem_limit_bytes=mib * 1024 * 1024)


def prepare_kernel(kernel_ref, split_ref, target_ref, beta_ref, *coef_refs):
    kernel, split = kernel_ref[...], split_ref[...]
    beta = 0.5 * (kernel + kernel.T)
    weight = 0.5 * (split + split.T)
    beta_ref[...] = beta.astype(BF16)
    rows = lax.broadcasted_iota(jnp.int32, (K, K), 0)
    cols = lax.broadcasted_iota(jnp.int32, (K, K), 1)
    count = jnp.where(cols < rows, 2.0, jnp.where(cols == rows, 1.0, 0.0))
    low = 0.5 * beta * weight * count
    high = 0.5 * beta * (1.0 - weight) * count
    target = jnp.where(cols <= rows, target_ref[...], 0)
    for block in range(BLOCKS):
        n = B * (block + 1)
        tiles = n * B // K
        parts = [[None] * tiles for _ in range(3)]
        for jj in range(B):
            j = B * block + jj
            for which, array in enumerate((low, high, target)):
                row = array[j : j + 1]
                offset = jj * n
                first, shift = offset // K, offset % K
                if shift:
                    row = pltpu.roll(row, shift, 1)
                lane = cols[:1]
                pieces = [(first, row)]
                if shift + n > K:
                    zero = jnp.zeros_like(row)
                    pieces = [(first, jnp.where(lane >= shift, row, zero)), (first + 1, jnp.where(lane < shift, row, zero))]
                for tile, piece in pieces:
                    had = parts[which][tile]
                    parts[which][tile] = piece if had is None else had + piece
        top = K - B * block
        ks = lax.broadcasted_iota(jnp.int32, (top, K), 0) + B * block
        for tile in range(tiles):
            a, b, t = (parts[which][tile] for which in range(3))
            value = jnp.where(ks == t, a, jnp.where(ks == t + 1, b, 0.0))
            coef_refs[block][:, tile * K : (tile + 1) * K] = value.astype(BF16)


def prepare(kernel, split, target):
    shapes = [jax.ShapeDtypeStruct((K, K), BF16)]
    shapes += [jax.ShapeDtypeStruct((K - B * b, B * B * (b + 1)), BF16) for b in range(BLOCKS)]
    return pl.pallas_call(
        prepare_kernel,
        out_shape=shapes,
        in_specs=[VMEM] * 3,
        out_specs=[VMEM] * (BLOCKS + 1),
        compiler_params=params(16),
        name="prepare",
    )(kernel, split, target)


def reaction(planes, beta, coefs, pair_ref):
    x = jnp.concatenate(planes, axis=1) if len(planes) > 1 else planes[0]
    width = x.shape[1]
    low = x.astype(BF16)
    total = None
    for block in range(BLOCKS):
        n = B * (block + 1)
        for jj in range(B):
            j = B * block + jj
            factor = jnp.broadcast_to(x[j : j + 1], (B, width)).astype(BF16)
            for part in range(block + 1):
                at = jj * n + B * part
                pair_ref[at : at + B, :width] = low[B * part : B * (part + 1)] * factor
        gain = jnp.dot(coefs[block][...], pair_ref[: B * n, :width], preferred_element_type=F32)
        if block == 0:
            total = gain
        else:
            total = jnp.concatenate([total[: B * block], total[B * block :] + gain], axis=0)
    rate = jnp.dot(beta[...], low, preferred_element_type=F32)
    change = total - x * rate
    return [change[:, CELLS * p : CELLS * (p + 1)] for p in range(len(planes))]


def moved(before, here, after, speed_before, speed_here):
    out = jnp.maximum(speed_here, 0.0) * here + jnp.minimum(speed_here, 0.0) * after
    came = jnp.maximum(speed_before, 0.0) * before + jnp.minimum(speed_before, 0.0) * here
    return here - (out - came)


def inner_kernel(core_ref, chip_ref, beta_ref, *refs):
    coefs, outs, (pair_ref, speed_ref) = refs[:BLOCKS], refs[BLOCKS:-2], refs[-2:]
    react1_ref, state1_ref, react2_ref, state2_ref, react3_ref = outs
    core = core_ref[0]
    sign = (1 - 2 * core).astype(F32)
    planes = [chip_ref[5 * core + (1 - 2 * core) * p, :K] for p in range(6)]
    for p in range(6):
        speed_ref[p : p + 1] = chip_ref[p, K : K + 1] + chip_ref[p, K + 1 : K + 2] * (1.0 / 2048.0)
    faces = [sign * speed_ref[pl.ds(4 * core + (1 - 2 * core) * f, 1)] for f in range(5)]
    changes = reaction(planes, beta_ref, coefs, pair_ref)
    react1_ref[0], react1_ref[1] = changes[0], changes[5]
    planes = [moved(*planes[p - 1 : p + 2], faces[p - 1], faces[p]) + changes[p] for p in range(1, 5)]
    for p in range(4):
        state1_ref[p] = planes[p]
    changes = reaction(planes, beta_ref, coefs, pair_ref)
    react2_ref[0], react2_ref[1] = changes[0], changes[3]
    planes = [moved(*planes[p - 1 : p + 2], faces[p], faces[p + 1]) + changes[p] for p in range(1, 3)]
    changes = reaction(planes, beta_ref, coefs, pair_ref)
    for p in range(2):
        state2_ref[p] = planes[p]
        react3_ref[p] = changes[p]


def outer_kernel(core_ref, chip_ref, far_ref, near_ref, react1_ref, state1_ref, react2_ref, state2_ref, react3_ref, beta_ref, *refs):
    coefs, out_ref, pair_ref, speed_ref = refs[:BLOCKS], refs[BLOCKS], refs[BLOCKS + 1], refs[BLOCKS + 2]
    core = core_ref[0]
    step = 1 - 2 * core
    sign = step.astype(F32)

    def speed(ref, p):
        return ref[p, K : K + 1] + ref[p, K + 1 : K + 2] * (1.0 / 2048.0)

    for p in range(4):
        speed_ref[p : p + 1] = speed(far_ref, 3 * core + step * p)
    for p in range(6):
        speed_ref[4 + p : 5 + p] = speed(chip_ref, 5 * core + step * p)
    speed_ref[10:11] = near_ref[K : K + 1] + near_ref[K + 1 : K + 2] * (1.0 / 2048.0)
    faces = [sign * speed_ref[pl.ds(core + f, 1)] for f in range(10)]

    def advanced(state, change, w):
        return moved(state[w - 1], state[w], state[w + 1], faces[w - 1], faces[w]) + change[w]

    state = {w: far_ref[3 * core + step * w, :K] for w in range(4)}
    state.update({4 + p: chip_ref[5 * core + step * p, :K] for p in range(6)})
    state[10] = near_ref[:K]
    known_changes = [{4: react1_ref[0], 9: react1_ref[1]}, {5: react2_ref[0], 8: react2_ref[1]}, {6: react3_ref[0], 7: react3_ref[1]}, {}]
    known_states = [{5 + p: state1_ref[p] for p in range(4)}, {6 + p: state2_ref[p] for p in range(2)}, {}, {}]
    for t in range(STEPS):
        reacting = range(t + 1, t + 4)
        change = dict(zip(reacting, reaction([state[w] for w in reacting], beta_ref, coefs, pair_ref)))
        change.update(known_changes[t])
        after = dict(known_states[t])
        for w in range(t + 1, 10 - t):
            if w not in after:
                after[w] = advanced(state, change, w)
        state = after
    for p in range(3):
        value = state[4 + p] * (1.0 / 512.0)
        for d in range(16):
            out_ref[d, 2 * core + step * p] = value[8 * d : 8 * d + 8]


def scratch(planes, rows):
    return [pltpu.VMEM((2048, planes * CELLS), BF16)] + [pltpu.VMEM((r, CELLS), F32) for r in rows]


def cost(planes):
    return pl.CostEstimate(flops=2 * K * 9216 * CELLS * planes, bytes_accessed=3000000, transcendentals=0)


def on_device(density, velocity, kernel, split, target):
    core = lax.axis_index("core").astype(jnp.int32)
    beta, *coefs = prepare(kernel, split, target)
    blocks = density.reshape(3, 8, 16, CELLS).transpose(2, 0, 1, 3).astype(F16)
    blocks = lax.all_to_all(blocks, SECT, split_axis=0, concat_axis=0, tiled=True)
    speed = lax.dynamic_slice_in_dim(velocity, lax.axis_index(SECT) * CELLS, CELLS, 1)
    high = speed.astype(F16)
    rest = ((speed - high.astype(F32)) * 2048.0).astype(F16)
    own = blocks.transpose(1, 0, 2, 3).reshape(3, K, CELLS)
    own = jnp.concatenate([own, high[:, None], rest[:, None], jnp.zeros((3, 14, CELLS), F16)], axis=1)
    side = [((s + 2) % 32, s) if s % 2 == 0 else (s, (s + 2) % 32) for s in range(32)]
    near = lax.ppermute(lax.dynamic_index_in_dim(own, 2 * core, 0, keepdims=False), SPACE, side)
    chip = lax.all_gather(own, "core", axis=0, tiled=True)
    edge = lax.dynamic_slice_in_dim(chip, 2 * core, 4, 0)
    pairs = [(s, (s + 1) % 32) for s in range(1, 32, 2)]
    far = lax.ppermute(edge, SPACE, pairs + [(b, a) for a, b in pairs])
    chip = chip.astype(F32)
    core = core.reshape(1)
    plane = lambda n: jax.ShapeDtypeStruct((n, K, CELLS), F32)
    inner = pl.pallas_call(
        inner_kernel,
        out_shape=[plane(2), plane(4), plane(2), plane(2), plane(2)],
        in_specs=[SMEM] + [VMEM] * (2 + BLOCKS),
        out_specs=[VMEM] * 5,
        scratch_shapes=scratch(6, (8,)),
        compiler_params=params(24),
        cost_estimate=cost(12),
        name="inner",
    )(core, chip, beta, *coefs)
    blocks = pl.pallas_call(
        outer_kernel,
        out_shape=jax.ShapeDtypeStruct((16, 3, 8, CELLS), F32),
        in_specs=[SMEM] + [VMEM] * (9 + BLOCKS),
        out_specs=VMEM,
        scratch_shapes=scratch(3, (16,)),
        compiler_params=params(24),
        cost_estimate=cost(12),
        name="outer",
    )(core, chip, far.astype(F32), near.astype(F32), *inner, beta, *coefs)
    blocks = lax.all_to_all(blocks.astype(F16), SECT, split_axis=0, concat_axis=0, tiled=True)
    return blocks.transpose(1, 2, 0, 3).reshape(density.shape).astype(F32) * 512.0


def solution(mesh):
    torus = Mesh(mesh.devices.reshape(16, 2, 2, 8), ("chip", "core", "zl", "y"))
    return jax.shard_map(
        on_device,
        mesh=torus,
        in_specs=(P(SPACE, SECT, None), P(SPACE, None), P(), P(), P()),
        out_specs=P(SPACE, SECT, None),
        check_vma=False,
    )
```

```python
import jax
import jax.numpy as jnp
from jax import lax
from jax.experimental import pallas as pl
from jax.experimental.pallas import tpu as pltpu
from jax.sharding import Mesh
from jax.sharding import PartitionSpec as P

K = 128
CELLS = 128
BLOCKS = 8
B = 16
START = [K * b * (b + 1) for b in range(BLOCKS + 1)]
PAIRS = START[BLOCKS]
SECT = ("zl", "y")
SPACE = ("chip", "core")
STEPS = 4
VMEM = pl.BlockSpec(memory_space=pltpu.VMEM)
SMEM = pl.BlockSpec(memory_space=pltpu.SMEM)
F16 = jnp.float16
F32 = jnp.float32
BF16 = jnp.bfloat16


def params(mib):
    return pltpu.CompilerParams(vmem_limit_bytes=mib * 1024 * 1024)


def prepare_kernel(table_ref, beta_ref, coef_ref):
    kernel, split = table_ref[:K], table_ref[K : 2 * K]
    beta = 0.5 * (kernel + kernel.T)
    weight = 0.5 * (split + split.T)
    beta_ref[...] = beta.astype(BF16)
    rows = lax.broadcasted_iota(jnp.int32, (K, K), 0)
    cols = lax.broadcasted_iota(jnp.int32, (K, K), 1)
    count = jnp.where(cols < rows, 2.0, jnp.where(cols == rows, 1.0, 0.0))
    low = 0.5 * beta * weight * count
    high = 0.5 * beta * (1.0 - weight) * count
    target = jnp.where(cols <= rows, table_ref[2 * K :], 0.0).astype(jnp.int32)
    for block in range(BLOCKS):
        n = B * (block + 1)
        tiles = n * B // K
        parts = [[None] * tiles for _ in range(3)]
        for jj in range(B):
            j = B * block + jj
            for which, array in enumerate((low, high, target)):
                row = array[j : j + 1]
                offset = jj * n
                first, shift = offset // K, offset % K
                if shift:
                    row = pltpu.roll(row, shift, 1)
                lane = cols[:1]
                pieces = [(first, row)]
                if shift + n > K:
                    zero = jnp.zeros_like(row)
                    pieces = [(first, jnp.where(lane >= shift, row, zero)), (first + 1, jnp.where(lane < shift, row, zero))]
                for tile, piece in pieces:
                    had = parts[which][tile]
                    parts[which][tile] = piece if had is None else had + piece
        top = K - B * block
        ks = lax.broadcasted_iota(jnp.int32, (top, K), 0) + B * block
        for tile in range(tiles):
            a, b, t = (parts[which][tile] for which in range(3))
            value = jnp.where(ks == t, a, jnp.where(ks == t + 1, b, 0.0))
            at = START[block] + tile * K
            coef_ref[K - top :, at : at + K] = value.astype(BF16)
            if block:
                coef_ref[: K - top, at : at + K] = jnp.zeros((K - top, K), BF16)


def prepare(kernel, split, target):
    shapes = [jax.ShapeDtypeStruct((K, K), BF16), jax.ShapeDtypeStruct((K, PAIRS), BF16)]
    return pl.pallas_call(
        prepare_kernel,
        out_shape=shapes,
        in_specs=[VMEM],
        out_specs=[VMEM] * 2,
        compiler_params=params(16),
        name="prepare",
    )(jnp.concatenate([kernel, split, target.astype(F32)]))


def reaction(planes, beta, coef, pair_ref):
    x = jnp.concatenate(planes, axis=1) if len(planes) > 1 else planes[0]
    width = x.shape[1]
    low = x.astype(BF16)
    for block in range(BLOCKS):
        n = B * (block + 1)
        for jj in range(B):
            j = B * block + jj
            factor = jnp.broadcast_to(x[j : j + 1], (B, width)).astype(BF16)
            for part in range(block + 1):
                at = START[block] + jj * n + B * part
                pair_ref[at : at + B, :width] = low[B * part : B * (part + 1)] * factor
    gain = jnp.dot(coef[...], pair_ref[:, :width], preferred_element_type=F32)
    rate = jnp.dot(beta[...], low, preferred_element_type=F32)
    change = gain - x * rate
    return [change[:, CELLS * p : CELLS * (p + 1)] for p in range(len(planes))]


def moved(before, here, after, speed_before, speed_here):
    out = jnp.maximum(speed_here, 0.0) * here + jnp.minimum(speed_here, 0.0) * after
    came = jnp.maximum(speed_before, 0.0) * before + jnp.minimum(speed_before, 0.0) * here
    return here - (out - came)


def inner_kernel(core_ref, chip_ref, beta_ref, coef_ref, *refs):
    react1_ref, state1_ref, react2_ref, state2_ref, react3_ref, pair_ref, speed_ref = refs
    core = core_ref[0]
    sign = (1 - 2 * core).astype(F32)
    planes = [chip_ref[5 * core + (1 - 2 * core) * p, :K] for p in range(6)]
    for p in range(6):
        speed_ref[p : p + 1] = chip_ref[p, K : K + 1] + chip_ref[p, K + 1 : K + 2] * (1.0 / 2048.0)
    faces = [sign * speed_ref[pl.ds(4 * core + (1 - 2 * core) * f, 1)] for f in range(5)]
    changes = reaction(planes, beta_ref, coef_ref, pair_ref)
    react1_ref[0], react1_ref[1] = changes[0], changes[5]
    planes = [moved(*planes[p - 1 : p + 2], faces[p - 1], faces[p]) + changes[p] for p in range(1, 5)]
    for p in range(4):
        state1_ref[p] = planes[p]
    changes = reaction(planes, beta_ref, coef_ref, pair_ref)
    react2_ref[0], react2_ref[1] = changes[0], changes[3]
    planes = [moved(*planes[p - 1 : p + 2], faces[p], faces[p + 1]) + changes[p] for p in range(1, 3)]
    changes = reaction(planes, beta_ref, coef_ref, pair_ref)
    for p in range(2):
        state2_ref[p] = planes[p]
        react3_ref[p] = changes[p]


def outer_kernel(core_ref, chip_ref, far_ref, near_ref, react1_ref, state1_ref, react2_ref, state2_ref, react3_ref, beta_ref, coef_ref, out_ref, pair_ref, speed_ref):
    core = core_ref[0]
    step = 1 - 2 * core
    sign = step.astype(F32)

    def speed(ref, p):
        return ref[p, K : K + 1] + ref[p, K + 1 : K + 2] * (1.0 / 2048.0)

    for p in range(4):
        speed_ref[p : p + 1] = speed(far_ref, 3 * core + step * p)
    for p in range(6):
        speed_ref[4 + p : 5 + p] = speed(chip_ref, 5 * core + step * p)
    speed_ref[10:11] = near_ref[K : K + 1] + near_ref[K + 1 : K + 2] * (1.0 / 2048.0)
    faces = [sign * speed_ref[pl.ds(core + f, 1)] for f in range(10)]

    def advanced(state, change, w):
        return moved(state[w - 1], state[w], state[w + 1], faces[w - 1], faces[w]) + change[w]

    state = {w: far_ref[3 * core + step * w, :K] for w in range(4)}
    state.update({4 + p: chip_ref[5 * core + step * p, :K] for p in range(6)})
    state[10] = near_ref[:K]
    known_changes = [{4: react1_ref[0], 9: react1_ref[1]}, {5: react2_ref[0], 8: react2_ref[1]}, {6: react3_ref[0], 7: react3_ref[1]}, {}]
    known_states = [{5 + p: state1_ref[p] for p in range(4)}, {6 + p: state2_ref[p] for p in range(2)}, {}, {}]
    for t in range(STEPS):
        reacting = range(t + 1, t + 4)
        change = dict(zip(reacting, reaction([state[w] for w in reacting], beta_ref, coef_ref, pair_ref)))
        change.update(known_changes[t])
        after = dict(known_states[t])
        for w in range(t + 1, 10 - t):
            if w not in after:
                after[w] = advanced(state, change, w)
        state = after
    for p in range(3):
        value = state[4 + p] * (1.0 / 512.0)
        for d in range(16):
            out_ref[d, 2 * core + step * p] = value[8 * d : 8 * d + 8]


def scratch(planes, rows):
    return [pltpu.VMEM((PAIRS, planes * CELLS), BF16)] + [pltpu.VMEM((r, CELLS), F32) for r in rows]


def cost(planes):
    return pl.CostEstimate(flops=2 * K * 9216 * CELLS * planes, bytes_accessed=3000000, transcendentals=0)


def on_device(density, velocity, kernel, split, target):
    core = lax.axis_index("core").astype(jnp.int32)
    beta, coef = prepare(kernel, split, target)
    blocks = density.reshape(3, 8, 16, CELLS).astype(F16)
    blocks = lax.all_to_all(blocks, SECT, split_axis=2, concat_axis=2, tiled=True)
    speed = lax.dynamic_slice_in_dim(velocity, lax.axis_index(SECT) * CELLS, CELLS, 1)
    high = speed.astype(F16)
    rest = ((speed - high.astype(F32)) * 2048.0).astype(F16)
    own = blocks.transpose(0, 2, 1, 3).reshape(3, K, CELLS)
    own = jnp.concatenate([own, high[:, None], rest[:, None], jnp.zeros((3, 14, CELLS), F16)], axis=1)
    chip = lax.all_gather(own, "core", axis=0, tiled=True)
    edge = lax.dynamic_slice_in_dim(chip, 2 * core, 4, 0)
    pairs = [(s, (s + 1) % 32) for s in range(1, 32, 2)]
    far = lax.ppermute(edge, SPACE, pairs + [(b, a) for a, b in pairs])
    near = lax.all_gather(lax.dynamic_index_in_dim(far, 3 * (1 - core), 0, keepdims=False), "core", axis=0)
    near = lax.dynamic_index_in_dim(near, 1 - core, 0, keepdims=False)
    chip = chip.astype(F32)
    core = core.reshape(1)
    plane = lambda n: jax.ShapeDtypeStruct((n, K, CELLS), F32)
    inner = pl.pallas_call(
        inner_kernel,
        out_shape=[plane(2), plane(4), plane(2), plane(2), plane(2)],
        in_specs=[SMEM] + [VMEM] * 3,
        out_specs=[VMEM] * 5,
        scratch_shapes=scratch(6, (8,)),
        compiler_params=params(24),
        cost_estimate=cost(12),
        name="inner",
    )(core, chip, beta, coef)
    blocks = pl.pallas_call(
        outer_kernel,
        out_shape=jax.ShapeDtypeStruct((16, 3, 8, CELLS), F32),
        in_specs=[SMEM] + [VMEM] * 10,
        out_specs=VMEM,
        scratch_shapes=scratch(3, (16,)),
        compiler_params=params(24),
        cost_estimate=cost(12),
        name="outer",
    )(core, chip, far.astype(F32), near.astype(F32), *inner, beta, coef)
    blocks = lax.all_to_all(blocks.astype(F16), SECT, split_axis=0, concat_axis=0, tiled=True)
    return blocks.transpose(1, 2, 0, 3).reshape(density.shape).astype(F32) * 512.0


def solution(mesh):
    torus = Mesh(mesh.devices.reshape(16, 2, 2, 8), ("chip", "core", "zl", "y"))
    return jax.shard_map(
        on_device,
        mesh=torus,
        in_specs=(P(SPACE, SECT, None), P(SPACE, None), P(), P(), P()),
        out_specs=P(SPACE, SECT, None),
        check_vma=False,
    )
```

```python
import functools

import jax
import jax.numpy as jnp
from jax import lax
from jax.experimental import pallas as pl
from jax.experimental.pallas import tpu as pltpu
from jax.sharding import Mesh
from jax.sharding import PartitionSpec as P

K = 128
CELLS = 128
BLOCKS = 8
B = 16
START = [K * b * (b + 1) for b in range(BLOCKS + 1)]
PAIRS = START[BLOCKS]
SECT = ("zl", "y")
SPACE = ("chip", "core")
STEPS = 4
VMEM = pl.BlockSpec(memory_space=pltpu.VMEM)
SMEM = pl.BlockSpec(memory_space=pltpu.SMEM)
F16 = jnp.float16
F32 = jnp.float32
BF16 = jnp.bfloat16


def params(mib):
    return pltpu.CompilerParams(vmem_limit_bytes=mib * 1024 * 1024)


def prepare_kernel(table_ref, beta_ref, coef_ref):
    kernel, split = table_ref[:K], table_ref[K : 2 * K]
    beta = 0.5 * (kernel + kernel.T)
    weight = 0.5 * (split + split.T)
    beta_ref[...] = beta.astype(BF16)
    rows = lax.broadcasted_iota(jnp.int32, (K, K), 0)
    cols = lax.broadcasted_iota(jnp.int32, (K, K), 1)
    count = jnp.where(cols < rows, 2.0, jnp.where(cols == rows, 1.0, 0.0))
    low = 0.5 * beta * weight * count
    high = 0.5 * beta * (1.0 - weight) * count
    target = jnp.where(cols <= rows, table_ref[2 * K :], 0.0).astype(jnp.int32)
    for block in range(BLOCKS):
        n = B * (block + 1)
        tiles = n * B // K
        parts = [[None] * tiles for _ in range(3)]
        for jj in range(B):
            j = B * block + jj
            for which, array in enumerate((low, high, target)):
                row = array[j : j + 1]
                offset = jj * n
                first, shift = offset // K, offset % K
                if shift:
                    row = pltpu.roll(row, shift, 1)
                lane = cols[:1]
                pieces = [(first, row)]
                if shift + n > K:
                    zero = jnp.zeros_like(row)
                    pieces = [(first, jnp.where(lane >= shift, row, zero)), (first + 1, jnp.where(lane < shift, row, zero))]
                for tile, piece in pieces:
                    had = parts[which][tile]
                    parts[which][tile] = piece if had is None else had + piece
        top = K - B * block
        ks = lax.broadcasted_iota(jnp.int32, (top, K), 0) + B * block
        for tile in range(tiles):
            a, b, t = (parts[which][tile] for which in range(3))
            value = jnp.where(ks == t, a, jnp.where(ks == t + 1, b, 0.0))
            at = START[block] + tile * K
            coef_ref[K - top :, at : at + K] = value.astype(BF16)
            if block:
                coef_ref[: K - top, at : at + K] = jnp.zeros((K - top, K), BF16)


def prepare(kernel, split, target):
    shapes = [jax.ShapeDtypeStruct((K, K), BF16), jax.ShapeDtypeStruct((K, PAIRS), BF16)]
    return pl.pallas_call(
        prepare_kernel,
        out_shape=shapes,
        in_specs=[VMEM],
        out_specs=[VMEM] * 2,
        compiler_params=params(16),
        name="prepare",
    )(jnp.concatenate([kernel, split, target.astype(F32)]))


def reaction(planes, beta, coef, pair_ref):
    x = jnp.concatenate(planes, axis=1) if len(planes) > 1 else planes[0]
    width = x.shape[1]
    low = x.astype(BF16)
    gain = None
    for group in ((range(4), range(4, 6), range(6, 8)) if len(planes) == 3 else (range(BLOCKS),)):
        for block in group:
            n = B * (block + 1)
            for jj in range(B):
                j = B * block + jj
                factor = jnp.broadcast_to(x[j : j + 1], (B, width)).astype(BF16)
                for part in range(block + 1):
                    at = START[block] + jj * n + B * part
                    pair_ref[at : at + B, :width] = low[B * part : B * (part + 1)] * factor
        first, begin, end = B * group[0], START[group[0]], START[group[-1] + 1]
        some = jnp.dot(coef[first:, begin:end], pair_ref[begin:end, :width], preferred_element_type=F32)
        gain = some if gain is None else jnp.concatenate([gain[:first], gain[first:] + some], axis=0)
    rate = jnp.dot(beta[...], low, preferred_element_type=F32)
    change = gain - x * rate
    return [change[:, CELLS * p : CELLS * (p + 1)] for p in range(len(planes))]


def moved(before, here, after, speed_before, speed_here):
    out = jnp.maximum(speed_here, 0.0) * here + jnp.minimum(speed_here, 0.0) * after
    came = jnp.maximum(speed_before, 0.0) * before + jnp.minimum(speed_before, 0.0) * here
    return here - (out - came)


def inner_kernel(turn, place_ref, chip_ref, beta_ref, coef_ref, *refs):
    @pl.when(place_ref[1] == turn)
    def _():
        inner(place_ref[0], chip_ref, beta_ref, coef_ref, *refs[-7:])


def inner(core, chip_ref, beta_ref, coef_ref, react1_ref, state1_ref, react2_ref, state2_ref, react3_ref, pair_ref, speed_ref):
    sign = (1 - 2 * core).astype(F32)
    planes = [chip_ref[5 * core + (1 - 2 * core) * p, :K] for p in range(6)]
    for p in range(6):
        speed_ref[p : p + 1] = chip_ref[p, K : K + 1] + chip_ref[p, K + 1 : K + 2] * (1.0 / 2048.0)
    faces = [sign * speed_ref[pl.ds(4 * core + (1 - 2 * core) * f, 1)] for f in range(5)]
    changes = reaction(planes, beta_ref, coef_ref, pair_ref)
    react1_ref[0], react1_ref[1] = changes[0], changes[5]
    planes = [moved(*planes[p - 1 : p + 2], faces[p - 1], faces[p]) + changes[p] for p in range(1, 5)]
    for p in range(4):
        state1_ref[p] = planes[p]
    changes = reaction(planes, beta_ref, coef_ref, pair_ref)
    react2_ref[0], react2_ref[1] = changes[0], changes[3]
    planes = [moved(*planes[p - 1 : p + 2], faces[p], faces[p + 1]) + changes[p] for p in range(1, 3)]
    changes = reaction(planes, beta_ref, coef_ref, pair_ref)
    for p in range(2):
        state2_ref[p] = planes[p]
        react3_ref[p] = changes[p]


def outer_kernel(place_ref, chip_ref, far_ref, near_ref, react1_ref, state1_ref, react2_ref, state2_ref, react3_ref, beta_ref, coef_ref, out_ref, pair_ref, speed_ref):
    core = place_ref[0]
    step = 1 - 2 * core
    sign = step.astype(F32)

    def speed(ref, p):
        return ref[p, K : K + 1] + ref[p, K + 1 : K + 2] * (1.0 / 2048.0)

    for p in range(4):
        speed_ref[p : p + 1] = speed(far_ref, 3 * core + step * p)
    for p in range(6):
        speed_ref[4 + p : 5 + p] = speed(chip_ref, 5 * core + step * p)
    speed_ref[10:11] = near_ref[K : K + 1] + near_ref[K + 1 : K + 2] * (1.0 / 2048.0)
    faces = [sign * speed_ref[pl.ds(core + f, 1)] for f in range(10)]

    def advanced(state, change, w):
        return moved(state[w - 1], state[w], state[w + 1], faces[w - 1], faces[w]) + change[w]

    state = {w: far_ref[3 * core + step * w, :K] for w in range(4)}
    state.update({4 + p: chip_ref[5 * core + step * p, :K] for p in range(6)})
    state[10] = near_ref[:K]
    known_changes = [{4: react1_ref[0], 9: react1_ref[1]}, {5: react2_ref[0], 8: react2_ref[1]}, {6: react3_ref[0], 7: react3_ref[1]}, {}]
    known_states = [{5 + p: state1_ref[p] for p in range(4)}, {6 + p: state2_ref[p] for p in range(2)}, {}, {}]
    for t in range(STEPS):
        reacting = range(t + 1, t + 4)
        change = dict(zip(reacting, reaction([state[w] for w in reacting], beta_ref, coef_ref, pair_ref)))
        change.update(known_changes[t])
        after = dict(known_states[t])
        for w in range(t + 1, 10 - t):
            if w not in after:
                after[w] = advanced(state, change, w)
        state = after
    for p in range(3):
        value = state[4 + p] * (1.0 / 512.0)
        for d in range(16):
            out_ref[d, 2 * core + step * p] = value[8 * d : 8 * d + 8]


def scratch(planes, rows):
    return [pltpu.VMEM((PAIRS, planes * CELLS), BF16)] + [pltpu.VMEM((r, CELLS), F32) for r in rows]


def cost(planes):
    return pl.CostEstimate(flops=2 * K * 9216 * CELLS * planes, bytes_accessed=3000000, transcendentals=0)


def react_inside(turn, place, chip, beta, coef, found):
    return pl.pallas_call(
        functools.partial(inner_kernel, turn),
        out_shape=[jax.ShapeDtypeStruct((n, K, CELLS), F32) for n in (2, 4, 2, 2, 2)],
        in_specs=[SMEM] + [VMEM] * (3 + len(found)),
        out_specs=[VMEM] * 5,
        scratch_shapes=scratch(6, (8,)),
        input_output_aliases={4 + n: n for n in range(len(found))},
        compiler_params=params(24),
        cost_estimate=cost(12),
        name=("before", "after")[turn],
    )(place, chip, beta, coef, *found)


def on_device(density, velocity, kernel, split, target):
    core = lax.axis_index("core").astype(jnp.int32)
    beta, coef = prepare(kernel, split, target)
    blocks = density.reshape(3, 8, 16, CELLS).astype(F16)
    blocks = lax.all_to_all(blocks, SECT, split_axis=2, concat_axis=2, tiled=True)
    speed = lax.dynamic_slice_in_dim(velocity, lax.axis_index(SECT) * CELLS, CELLS, 1)
    high = speed.astype(F16)
    rest = ((speed - high.astype(F32)) * 2048.0).astype(F16)
    own = blocks.transpose(0, 2, 1, 3).reshape(3, K, CELLS)
    own = jnp.concatenate([own, high[:, None], rest[:, None], jnp.zeros((3, 14, CELLS), F16)], axis=1)
    chip = lax.all_gather(own, "core", axis=0, tiled=True)
    place = jnp.stack([core, jnp.where(lax.axis_index("chip") % 4 < 2, 0, 1).astype(jnp.int32)])
    wide = chip.astype(F32)
    found = react_inside(0, place, wide, beta, coef, [])
    edge = lax.dynamic_slice_in_dim(chip, 2 * core, 4, 0)
    side = lax.dynamic_index_in_dim(own, 2 * core, 0, keepdims=False)
    edge, side, found = lax.optimization_barrier((edge, side, found))
    pairs = [(s, (s + 1) % 32) for s in range(1, 32, 2)]
    far = lax.ppermute(edge, SPACE, pairs + [(b, a) for a, b in pairs])
    near = lax.ppermute(side, SPACE, [((s + 2) % 32, s) if s % 2 == 0 else (s, (s + 2) % 32) for s in range(32)])
    found = react_inside(1, place, wide, beta, coef, found)
    blocks = pl.pallas_call(
        outer_kernel,
        out_shape=jax.ShapeDtypeStruct((16, 3, 8, CELLS), F32),
        in_specs=[SMEM] + [VMEM] * 10,
        out_specs=VMEM,
        scratch_shapes=scratch(3, (16,)),
        compiler_params=params(24),
        cost_estimate=cost(12),
        name="outer",
    )(place, wide, far.astype(F32), near.astype(F32), *found, beta, coef)
    blocks = lax.all_to_all(blocks.astype(F16), SECT, split_axis=0, concat_axis=0, tiled=True)
    return blocks.transpose(1, 2, 0, 3).reshape(density.shape).astype(F32) * 512.0


def solution(mesh):
    torus = Mesh(mesh.devices.reshape(16, 2, 2, 8), ("chip", "core", "zl", "y"))
    return jax.shard_map(
        on_device,
        mesh=torus,
        in_specs=(P(SPACE, SECT, None), P(SPACE, None), P(), P(), P()),
        out_specs=P(SPACE, SECT, None),
        check_vma=False,
    )
```

```python
import jax
import jax.numpy as jnp
from jax import lax
from jax.experimental import pallas as pl
from jax.experimental.pallas import tpu as pltpu
from jax.sharding import Mesh
from jax.sharding import PartitionSpec as P

K = 128
CELLS = 128
BLOCKS = 8
B = 16
START = [K * b * (b + 1) for b in range(BLOCKS + 1)]
PAIRS = START[BLOCKS]
SECT = ("zl", "y")
SPACE = ("chip", "core")
STEPS = 4
VMEM = pl.BlockSpec(memory_space=pltpu.VMEM)
SMEM = pl.BlockSpec(memory_space=pltpu.SMEM)
F16 = jnp.float16
F32 = jnp.float32
BF16 = jnp.bfloat16


def params(mib):
    return pltpu.CompilerParams(vmem_limit_bytes=mib * 1024 * 1024)


def prepare_kernel(table_ref, beta_ref, coef_ref):
    kernel, split = table_ref[:K], table_ref[K : 2 * K]
    beta = 0.5 * (kernel + kernel.T)
    weight = 0.5 * (split + split.T)
    beta_ref[...] = beta.astype(BF16)
    rows = lax.broadcasted_iota(jnp.int32, (K, K), 0)
    cols = lax.broadcasted_iota(jnp.int32, (K, K), 1)
    count = jnp.where(cols < rows, 2.0, jnp.where(cols == rows, 1.0, 0.0))
    low = 0.5 * beta * weight * count
    high = 0.5 * beta * (1.0 - weight) * count
    target = jnp.where(cols <= rows, table_ref[2 * K :], 0.0).astype(jnp.int32)
    for block in range(BLOCKS):
        n = B * (block + 1)
        tiles = n * B // K
        parts = [[None] * tiles for _ in range(3)]
        for jj in range(B):
            j = B * block + jj
            for which, array in enumerate((low, high, target)):
                row = array[j : j + 1]
                offset = jj * n
                first, shift = offset // K, offset % K
                if shift:
                    row = pltpu.roll(row, shift, 1)
                lane = cols[:1]
                pieces = [(first, row)]
                if shift + n > K:
                    zero = jnp.zeros_like(row)
                    pieces = [(first, jnp.where(lane >= shift, row, zero)), (first + 1, jnp.where(lane < shift, row, zero))]
                for tile, piece in pieces:
                    had = parts[which][tile]
                    parts[which][tile] = piece if had is None else had + piece
        top = K - B * block
        ks = lax.broadcasted_iota(jnp.int32, (top, K), 0) + B * block
        for tile in range(tiles):
            a, b, t = (parts[which][tile] for which in range(3))
            value = jnp.where(ks == t, a, jnp.where(ks == t + 1, b, 0.0))
            at = START[block] + tile * K
            coef_ref[K - top :, at : at + K] = value.astype(BF16)
            if block:
                coef_ref[: K - top, at : at + K] = jnp.zeros((K - top, K), BF16)


def prepare(kernel, split, target):
    shapes = [jax.ShapeDtypeStruct((K, K), BF16), jax.ShapeDtypeStruct((K, PAIRS), BF16)]
    return pl.pallas_call(
        prepare_kernel,
        out_shape=shapes,
        in_specs=[VMEM],
        out_specs=[VMEM] * 2,
        compiler_params=params(16),
        name="prepare",
    )(jnp.concatenate([kernel, split, target.astype(F32)]))


def reaction(planes, beta, coef, pair_ref):
    x = jnp.concatenate(planes, axis=1) if len(planes) > 1 else planes[0]
    width = x.shape[1]
    low = x.astype(BF16)
    for block in range(BLOCKS):
        n = B * (block + 1)
        for jj in range(B):
            j = B * block + jj
            factor = jnp.broadcast_to(x[j : j + 1], (B, width)).astype(BF16)
            for part in range(block + 1):
                at = START[block] + jj * n + B * part
                pair_ref[at : at + B, :width] = low[B * part : B * (part + 1)] * factor
    gain = jnp.dot(coef[...], pair_ref[:, :width], preferred_element_type=F32)
    rate = jnp.dot(beta[...], low, preferred_element_type=F32)
    change = gain - x * rate
    return [change[:, CELLS * p : CELLS * (p + 1)] for p in range(len(planes))]


def moved(before, here, after, speed_before, speed_here):
    out = jnp.maximum(speed_here, 0.0) * here + jnp.minimum(speed_here, 0.0) * after
    came = jnp.maximum(speed_before, 0.0) * before + jnp.minimum(speed_before, 0.0) * here
    return here - (out - came)


def inner_faces(core, chip_ref, speed_ref):
    sign = (1 - 2 * core).astype(F32)
    for p in range(6):
        speed_ref[p : p + 1] = chip_ref[p, K : K + 1] + chip_ref[p, K + 1 : K + 2] * (1.0 / 2048.0)
    return [sign * speed_ref[pl.ds(4 * core + (1 - 2 * core) * f, 1)] for f in range(5)]


def inner_first(core, chip_ref, beta_ref, coef_ref, react1_ref, state1_ref, pair_ref, speed_ref):
    faces = inner_faces(core, chip_ref, speed_ref)
    planes = [chip_ref[5 * core + (1 - 2 * core) * p, :K] for p in range(6)]
    changes = reaction(planes, beta_ref, coef_ref, pair_ref)
    react1_ref[0], react1_ref[1] = changes[0], changes[5]
    for p in range(1, 5):
        state1_ref[p - 1] = moved(*planes[p - 1 : p + 2], faces[p - 1], faces[p]) + changes[p]


def before_kernel(place_ref, chip_ref, beta_ref, coef_ref, react1_ref, state1_ref, pair_ref, speed_ref):
    @pl.when(place_ref[1] == 0)
    def _():
        inner_first(place_ref[0], chip_ref, beta_ref, coef_ref, react1_ref, state1_ref, pair_ref, speed_ref)


def after_kernel(place_ref, chip_ref, beta_ref, coef_ref, _, __, react1_ref, state1_ref, react2_ref, state2_ref, react3_ref, pair_ref, speed_ref):
    core = place_ref[0]

    @pl.when(place_ref[1] == 1)
    def _():
        inner_first(core, chip_ref, beta_ref, coef_ref, react1_ref, state1_ref, pair_ref, speed_ref)

    faces = inner_faces(core, chip_ref, speed_ref)
    planes = [state1_ref[p] for p in range(4)]
    changes = reaction(planes, beta_ref, coef_ref, pair_ref)
    react2_ref[0], react2_ref[1] = changes[0], changes[3]
    planes = [moved(*planes[p - 1 : p + 2], faces[p], faces[p + 1]) + changes[p] for p in range(1, 3)]
    changes = reaction(planes, beta_ref, coef_ref, pair_ref)
    for p in range(2):
        state2_ref[p] = planes[p]
        react3_ref[p] = changes[p]


def outer_kernel(place_ref, chip_ref, far_ref, near_ref, react1_ref, state1_ref, react2_ref, state2_ref, react3_ref, beta_ref, coef_ref, out_ref, pair_ref, speed_ref):
    core = place_ref[0]
    step = 1 - 2 * core
    sign = step.astype(F32)

    def speed(ref, p):
        return ref[p, K : K + 1] + ref[p, K + 1 : K + 2] * (1.0 / 2048.0)

    for p in range(4):
        speed_ref[p : p + 1] = speed(far_ref, 3 * core + step * p)
    for p in range(6):
        speed_ref[4 + p : 5 + p] = speed(chip_ref, 5 * core + step * p)
    speed_ref[10:11] = near_ref[K : K + 1] + near_ref[K + 1 : K + 2] * (1.0 / 2048.0)
    faces = [sign * speed_ref[pl.ds(core + f, 1)] for f in range(10)]

    def advanced(state, change, w):
        return moved(state[w - 1], state[w], state[w + 1], faces[w - 1], faces[w]) + change[w]

    state = {w: far_ref[3 * core + step * w, :K] for w in range(4)}
    state.update({4 + p: chip_ref[5 * core + step * p, :K] for p in range(6)})
    state[10] = near_ref[:K]
    known_changes = [{4: react1_ref[0], 9: react1_ref[1]}, {5: react2_ref[0], 8: react2_ref[1]}, {6: react3_ref[0], 7: react3_ref[1]}, {}]
    known_states = [{5 + p: state1_ref[p] for p in range(4)}, {6 + p: state2_ref[p] for p in range(2)}, {}, {}]
    for t in range(STEPS):
        reacting = range(t + 1, t + 4)
        change = dict(zip(reacting, reaction([state[w] for w in reacting], beta_ref, coef_ref, pair_ref)))
        change.update(known_changes[t])
        after = dict(known_states[t])
        for w in range(t + 1, 10 - t):
            if w not in after:
                after[w] = advanced(state, change, w)
        state = after
    for p in range(3):
        value = state[4 + p] * (1.0 / 512.0)
        for d in range(16):
            out_ref[d, 2 * core + step * p] = value[8 * d : 8 * d + 8]


def scratch(planes, rows):
    return [pltpu.VMEM((PAIRS, planes * CELLS), BF16)] + [pltpu.VMEM((r, CELLS), F32) for r in rows]


def cost(planes):
    return pl.CostEstimate(flops=2 * K * 9216 * CELLS * planes, bytes_accessed=3000000, transcendentals=0)


def react_inside(kernel, place, chip, beta, coef, found, outs):
    return pl.pallas_call(
        kernel,
        out_shape=[jax.ShapeDtypeStruct((n, K, CELLS), F32) for n in outs],
        in_specs=[SMEM] + [VMEM] * (3 + len(found)),
        out_specs=[VMEM] * len(outs),
        scratch_shapes=scratch(6, (8,)),
        input_output_aliases={4 + n: n for n in range(len(found))},
        compiler_params=params(24),
        cost_estimate=cost(6),
        name=kernel.__name__.partition("_")[0],
    )(place, chip, beta, coef, *found)


def on_device(density, velocity, kernel, split, target):
    core = lax.axis_index("core").astype(jnp.int32)
    beta, coef = prepare(kernel, split, target)
    blocks = density.reshape(3, 8, 16, CELLS).astype(F16)
    blocks = lax.all_to_all(blocks, SECT, split_axis=2, concat_axis=2, tiled=True)
    speed = lax.dynamic_slice_in_dim(velocity, lax.axis_index(SECT) * CELLS, CELLS, 1)
    high = speed.astype(F16)
    rest = ((speed - high.astype(F32)) * 2048.0).astype(F16)
    own = blocks.transpose(0, 2, 1, 3).reshape(3, K, CELLS)
    own = jnp.concatenate([own, high[:, None], rest[:, None], jnp.zeros((3, 14, CELLS), F16)], axis=1)
    chip = lax.all_gather(own, "core", axis=0, tiled=True)
    place = jnp.stack([core, jnp.where(lax.axis_index("chip") % 4 < 2, 0, 1).astype(jnp.int32)])
    wide = chip.astype(F32)
    found = react_inside(before_kernel, place, wide, beta, coef, [], (2, 4))
    edge = lax.dynamic_slice_in_dim(chip, 2 * core, 4, 0)
    edge, found = lax.optimization_barrier((edge, found))
    pairs = [(s, (s + 1) % 32) for s in range(1, 32, 2)]
    far = lax.ppermute(edge, SPACE, pairs + [(b, a) for a, b in pairs])
    found = react_inside(after_kernel, place, wide, beta, coef, found, (2, 4, 2, 2, 2))
    near = lax.all_gather(lax.dynamic_index_in_dim(far, 3 * (1 - core), 0, keepdims=False), "core", axis=0)
    near = lax.dynamic_index_in_dim(near, 1 - core, 0, keepdims=False)
    blocks = pl.pallas_call(
        outer_kernel,
        out_shape=jax.ShapeDtypeStruct((16, 3, 8, CELLS), F32),
        in_specs=[SMEM] + [VMEM] * 10,
        out_specs=VMEM,
        scratch_shapes=scratch(3, (16,)),
        compiler_params=params(24),
        cost_estimate=cost(12),
        name="outer",
    )(place, wide, far.astype(F32), near.astype(F32), *found, beta, coef)
    blocks = lax.all_to_all(blocks.astype(F16), SECT, split_axis=0, concat_axis=0, tiled=True)
    return blocks.transpose(1, 2, 0, 3).reshape(density.shape).astype(F32) * 512.0


def solution(mesh):
    torus = Mesh(mesh.devices.reshape(16, 2, 2, 8), ("chip", "core", "zl", "y"))
    return jax.shard_map(
        on_device,
        mesh=torus,
        in_specs=(P(SPACE, SECT, None), P(SPACE, None), P(), P(), P()),
        out_specs=P(SPACE, SECT, None),
        check_vma=False,
    )
```

```python
import jax
import jax.numpy as jnp
from jax import lax
from jax.experimental import pallas as pl
from jax.experimental.pallas import tpu as pltpu
from jax.sharding import Mesh
from jax.sharding import PartitionSpec as P

K = 128
CELLS = 128
BLOCKS = 8
B = 16
START = [K * b * (b + 1) for b in range(BLOCKS + 1)]
PAIRS = START[BLOCKS]
SECT = ("zl", "y")
SPACE = ("chip", "core")
STEPS = 4
VMEM = pl.BlockSpec(memory_space=pltpu.VMEM)
SMEM = pl.BlockSpec(memory_space=pltpu.SMEM)
F16 = jnp.float16
F32 = jnp.float32
BF16 = jnp.bfloat16


def params(mib):
    return pltpu.CompilerParams(vmem_limit_bytes=mib * 1024 * 1024)


def prepare_kernel(table_ref, beta_ref, coef_ref):
    kernel, split = table_ref[:K], table_ref[K : 2 * K]
    beta = 0.5 * (kernel + kernel.T)
    weight = 0.5 * (split + split.T)
    beta_ref[...] = beta.astype(BF16)
    rows = lax.broadcasted_iota(jnp.int32, (K, K), 0)
    cols = lax.broadcasted_iota(jnp.int32, (K, K), 1)
    count = jnp.where(cols < rows, 2.0, jnp.where(cols == rows, 1.0, 0.0))
    low = 0.5 * beta * weight * count
    high = 0.5 * beta * (1.0 - weight) * count
    target = jnp.where(cols <= rows, table_ref[2 * K :], 0.0).astype(jnp.int32)
    for block in range(BLOCKS):
        n = B * (block + 1)
        tiles = n * B // K
        parts = [[None] * tiles for _ in range(3)]
        for jj in range(B):
            j = B * block + jj
            for which, array in enumerate((low, high, target)):
                row = array[j : j + 1]
                offset = jj * n
                first, shift = offset // K, offset % K
                if shift:
                    row = pltpu.roll(row, shift, 1)
                lane = cols[:1]
                pieces = [(first, row)]
                if shift + n > K:
                    zero = jnp.zeros_like(row)
                    pieces = [(first, jnp.where(lane >= shift, row, zero)), (first + 1, jnp.where(lane < shift, row, zero))]
                for tile, piece in pieces:
                    had = parts[which][tile]
                    parts[which][tile] = piece if had is None else had + piece
        top = K - B * block
        ks = lax.broadcasted_iota(jnp.int32, (top, K), 0) + B * block
        for tile in range(tiles):
            a, b, t = (parts[which][tile] for which in range(3))
            value = jnp.where(ks == t, a, jnp.where(ks == t + 1, b, 0.0))
            at = START[block] + tile * K
            coef_ref[K - top :, at : at + K] = value.astype(BF16)
            if block:
                coef_ref[: K - top, at : at + K] = jnp.zeros((K - top, K), BF16)


def prepare(kernel, split, target):
    shapes = [jax.ShapeDtypeStruct((K, K), BF16), jax.ShapeDtypeStruct((K, PAIRS), BF16)]
    return pl.pallas_call(
        prepare_kernel,
        out_shape=shapes,
        in_specs=[VMEM],
        out_specs=[VMEM] * 2,
        compiler_params=params(16),
        name="prepare",
    )(jnp.concatenate([kernel, split, target.astype(F32)]))


def reaction(planes, beta, coef, pair_ref):
    x = jnp.concatenate(planes, axis=1) if len(planes) > 1 else planes[0]
    width = x.shape[1]
    low = x.astype(BF16)
    gain = None
    for group in [range(BLOCKS)] if len(planes) > 3 else [[block] for block in range(BLOCKS)]:
        for block in group:
            n = B * (block + 1)
            for jj in range(B):
                j = B * block + jj
                factor = jnp.broadcast_to(x[j : j + 1], (B, width)).astype(BF16)
                for part in range(block + 1):
                    at = START[block] + jj * n + B * part
                    pair_ref[at : at + B, :width] = low[B * part : B * (part + 1)] * factor
        first, begin, end = B * group[0], START[group[0]], START[group[-1] + 1]
        some = jnp.dot(coef[first:, begin:end], pair_ref[begin:end, :width], preferred_element_type=F32)
        gain = some if gain is None else jnp.concatenate([gain[:first], gain[first:] + some], axis=0)
    rate = jnp.dot(beta[...], low, preferred_element_type=F32)
    change = gain - x * rate
    return [change[:, CELLS * p : CELLS * (p + 1)] for p in range(len(planes))]


def moved(before, here, after, speed_before, speed_here):
    out = jnp.maximum(speed_here, 0.0) * here + jnp.minimum(speed_here, 0.0) * after
    came = jnp.maximum(speed_before, 0.0) * before + jnp.minimum(speed_before, 0.0) * here
    return here - (out - came)


def inner_faces(core, chip_ref, speed_ref):
    sign = (1 - 2 * core).astype(F32)
    for p in range(6):
        speed_ref[p : p + 1] = chip_ref[p, K : K + 1] + chip_ref[p, K + 1 : K + 2] * (1.0 / 2048.0)
    return [sign * speed_ref[pl.ds(4 * core + (1 - 2 * core) * f, 1)] for f in range(5)]


def inner(core, chip_ref, beta_ref, coef_ref, found, pair_ref, speed_ref):
    react1_ref, state1_ref, react2_ref, state2_ref, react3_ref = found
    faces = inner_faces(core, chip_ref, speed_ref)
    planes = [chip_ref[5 * core + (1 - 2 * core) * p, :K] for p in range(6)]
    changes = reaction(planes, beta_ref, coef_ref, pair_ref)
    react1_ref[0], react1_ref[1] = changes[0], changes[5]
    planes = [moved(*planes[p - 1 : p + 2], faces[p - 1], faces[p]) + changes[p] for p in range(1, 5)]
    for p in range(4):
        state1_ref[p] = planes[p]
    changes = reaction(planes, beta_ref, coef_ref, pair_ref)
    react2_ref[0], react2_ref[1] = changes[0], changes[3]
    planes = [moved(*planes[p - 1 : p + 2], faces[p], faces[p + 1]) + changes[p] for p in range(1, 3)]
    changes = reaction(planes, beta_ref, coef_ref, pair_ref)
    for p in range(2):
        state2_ref[p] = planes[p]
        react3_ref[p] = changes[p]


def before_kernel(place_ref, chip_ref, beta_ref, coef_ref, *refs):
    @pl.when(place_ref[1] == 0)
    def _():
        inner(place_ref[0], chip_ref, beta_ref, coef_ref, refs[:5], refs[5], refs[6])


def outer_kernel(place_ref, chip_ref, beta_ref, coef_ref, far_ref, near_ref, *refs):
    out_ref, found = refs[5], refs[6:11]
    pair_ref, speed_ref, state_ref, change_ref = refs[11:]
    react1_ref, state1_ref, react2_ref, state2_ref, react3_ref = found
    core = place_ref[0]
    step = 1 - 2 * core
    sign = step.astype(F32)

    @pl.when(place_ref[1] == 1)
    def _():
        inner(core, chip_ref, beta_ref, coef_ref, found, pair_ref, speed_ref)

    def speed(ref, p):
        return ref[p, K : K + 1] + ref[p, K + 1 : K + 2] * (1.0 / 2048.0)

    for p in range(4):
        speed_ref[p : p + 1] = speed(far_ref, 3 * core + step * p)
        state_ref[0, p] = far_ref[3 * core + step * p, :K]
    for p in range(6):
        speed_ref[4 + p : 5 + p] = speed(chip_ref, 5 * core + step * p)
        state_ref[0, 4 + p] = chip_ref[5 * core + step * p, :K]
    speed_ref[10:11] = near_ref[K : K + 1] + near_ref[K + 1 : K + 2] * (1.0 / 2048.0)
    state_ref[0, 10] = near_ref[:K]

    known_changes = [
        {4: (react1_ref, 0), 9: (react1_ref, 1)},
        {5: (react2_ref, 0), 8: (react2_ref, 1)},
        {6: (react3_ref, 0), 7: (react3_ref, 1)},
        {},
    ]
    known_states = [{5 + p: (state1_ref, p) for p in range(4)}, {6 + p: (state2_ref, p) for p in range(2)}, {}, {}]

    def transport(t):
        now, later = t % 2, (t + 1) % 2
        faces = [sign * speed_ref[pl.ds(core + f, 1)] for f in range(10)]
        change = {t + 1 + p: (change_ref, p) for p in range(3)} | known_changes[t]
        for w in range(t + 1, 10 - t):
            if w in known_states[t]:
                ref, at = known_states[t][w]
                state_ref[later, w] = ref[at]
            else:
                ref, at = change[w]
                near = [state_ref[now, v] for v in (w - 1, w, w + 1)]
                state_ref[later, w] = moved(*near, faces[w - 1], faces[w]) + ref[at]

    def advance(t, _):
        half = lax.rem(t, 2)
        planes = [state_ref[half, t + 1 + p] for p in range(3)]
        for p, change in enumerate(reaction(planes, beta_ref, coef_ref, pair_ref)):
            change_ref[p] = change
        for at in range(STEPS):
            pl.when(t == at)(lambda at=at: transport(at))
        return 0

    lax.fori_loop(0, STEPS, advance, 0)
    for p in range(3):
        value = state_ref[STEPS % 2, 4 + p] * (1.0 / 512.0)
        for d in range(16):
            out_ref[d, 2 * core + step * p] = value[8 * d : 8 * d + 8]


def scratch(planes, rows):
    return [pltpu.VMEM((PAIRS, planes * CELLS), BF16)] + [pltpu.VMEM((r, CELLS), F32) for r in rows]


def cost(planes):
    return pl.CostEstimate(flops=2 * K * 9216 * CELLS * planes, bytes_accessed=3000000, transcendentals=0)


def on_device(density, velocity, kernel, split, target):
    core = lax.axis_index("core").astype(jnp.int32)
    beta, coef = prepare(kernel, split, target)
    blocks = density.reshape(3, 8, 16, CELLS).astype(F16)
    blocks = lax.all_to_all(blocks, SECT, split_axis=2, concat_axis=2, tiled=True)
    speed = lax.dynamic_slice_in_dim(velocity, lax.axis_index(SECT) * CELLS, CELLS, 1)
    high = speed.astype(F16)
    rest = ((speed - high.astype(F32)) * 2048.0).astype(F16)
    own = blocks.transpose(0, 2, 1, 3).reshape(3, K, CELLS)
    own = jnp.concatenate([own, high[:, None], rest[:, None], jnp.zeros((3, 14, CELLS), F16)], axis=1)
    chip = lax.all_gather(own, "core", axis=0, tiled=True)
    place = jnp.stack([core, jnp.where(lax.axis_index("chip") % 4 < 2, 0, 1).astype(jnp.int32)])
    wide = chip.astype(F32)
    shapes = [jax.ShapeDtypeStruct((n, K, CELLS), F32) for n in (2, 4, 2, 2, 2)]
    found = pl.pallas_call(
        before_kernel,
        out_shape=shapes,
        in_specs=[SMEM] + [VMEM] * 3,
        out_specs=[VMEM] * 5,
        scratch_shapes=scratch(6, (8,)),
        compiler_params=params(24),
        cost_estimate=cost(12),
        name="before",
    )(place, wide, beta, coef)
    edge = lax.dynamic_slice_in_dim(chip, 2 * core, 4, 0)
    edge, found = lax.optimization_barrier((edge, found))
    neighbours = [[s, (s + 1) % 32] for s in range(1, 32, 2)]
    far = lax.all_gather(edge, SPACE, axis=0, axis_index_groups=neighbours)
    far = lax.dynamic_index_in_dim(far, core, 0, keepdims=False)
    near = lax.all_gather(lax.dynamic_index_in_dim(far, 3 * (1 - core), 0, keepdims=False), "core", axis=0)
    near = lax.dynamic_index_in_dim(near, 1 - core, 0, keepdims=False)
    blocks, *_ = pl.pallas_call(
        outer_kernel,
        out_shape=[jax.ShapeDtypeStruct((16, 3, 8, CELLS), F32), *shapes],
        in_specs=[SMEM] + [VMEM] * 10,
        out_specs=[VMEM] * 6,
        scratch_shapes=scratch(6, (16,)) + [pltpu.VMEM((2, 11, K, CELLS), F32), pltpu.VMEM((3, K, CELLS), F32)],
        input_output_aliases={6 + n: 1 + n for n in range(5)},
        compiler_params=params(32),
        cost_estimate=cost(12),
        name="outer",
    )(place, wide, beta, coef, far.astype(F32), near.astype(F32), *found)
    blocks = lax.all_to_all(blocks.astype(F16), SECT, split_axis=0, concat_axis=0, tiled=True)
    return blocks.transpose(1, 2, 0, 3).reshape(density.shape).astype(F32) * 512.0


def solution(mesh):
    torus = Mesh(mesh.devices.reshape(16, 2, 2, 8), ("chip", "core", "zl", "y"))
    return jax.shard_map(
        on_device,
        mesh=torus,
        in_specs=(P(SPACE, SECT, None), P(SPACE, None), P(), P(), P()),
        out_specs=P(SPACE, SECT, None),
        check_vma=False,
    )
```

```python
import jax
import jax.numpy as jnp
from jax import lax
from jax.experimental import pallas as pl
from jax.experimental.pallas import tpu as pltpu
from jax.sharding import Mesh
from jax.sharding import PartitionSpec as P

K = 128
CELLS = 128
BLOCKS = 8
B = 16
START = [K * b * (b + 1) for b in range(BLOCKS + 1)]
PAIRS = START[BLOCKS]
SECT = ("zl", "y")
SPACE = ("chip", "core")
STEPS = 4
VMEM = pl.BlockSpec(memory_space=pltpu.VMEM)
SMEM = pl.BlockSpec(memory_space=pltpu.SMEM)
F16 = jnp.float16
F32 = jnp.float32
BF16 = jnp.bfloat16


def params(mib):
    return pltpu.CompilerParams(vmem_limit_bytes=mib * 1024 * 1024)


def prepare_kernel(table_ref, beta_ref, coef_ref):
    kernel, split = table_ref[:K], table_ref[K : 2 * K]
    beta = 0.5 * (kernel + kernel.T)
    weight = 0.5 * (split + split.T)
    beta_ref[...] = beta.astype(BF16)
    rows = lax.broadcasted_iota(jnp.int32, (K, K), 0)
    cols = lax.broadcasted_iota(jnp.int32, (K, K), 1)
    count = jnp.where(cols < rows, 2.0, jnp.where(cols == rows, 1.0, 0.0))
    low = 0.5 * beta * weight * count
    high = 0.5 * beta * (1.0 - weight) * count
    target = jnp.where(cols <= rows, table_ref[2 * K :], 0.0).astype(jnp.int32)
    for block in range(BLOCKS):
        n = B * (block + 1)
        tiles = n * B // K
        parts = [[None] * tiles for _ in range(3)]
        for jj in range(B):
            j = B * block + jj
            for which, array in enumerate((low, high, target)):
                row = array[j : j + 1]
                offset = jj * n
                first, shift = offset // K, offset % K
                if shift:
                    row = pltpu.roll(row, shift, 1)
                lane = cols[:1]
                pieces = [(first, row)]
                if shift + n > K:
                    zero = jnp.zeros_like(row)
                    pieces = [(first, jnp.where(lane >= shift, row, zero)), (first + 1, jnp.where(lane < shift, row, zero))]
                for tile, piece in pieces:
                    had = parts[which][tile]
                    parts[which][tile] = piece if had is None else had + piece
        top = K - B * block
        ks = lax.broadcasted_iota(jnp.int32, (top, K), 0) + B * block
        for tile in range(tiles):
            a, b, t = (parts[which][tile] for which in range(3))
            value = jnp.where(ks == t, a, jnp.where(ks == t + 1, b, 0.0))
            at = START[block] + tile * K
            coef_ref[K - top :, at : at + K] = value.astype(BF16)
            if block:
                coef_ref[: K - top, at : at + K] = jnp.zeros((K - top, K), BF16)


def prepare(kernel, split, target):
    shapes = [jax.ShapeDtypeStruct((K, K), BF16), jax.ShapeDtypeStruct((K, PAIRS), BF16)]
    return pl.pallas_call(
        prepare_kernel,
        out_shape=shapes,
        in_specs=[VMEM],
        out_specs=[VMEM] * 2,
        compiler_params=params(16),
        name="prepare",
    )(jnp.concatenate([kernel, split, target.astype(F32)]))


def reaction(planes, beta, coef, pair_ref):
    x = jnp.concatenate(planes, axis=1) if len(planes) > 1 else planes[0]
    width = x.shape[1]
    low = x.astype(BF16)
    gain = None
    for group in [range(BLOCKS)] if len(planes) > 3 else [[block] for block in range(BLOCKS)]:
        for block in group:
            n = B * (block + 1)
            for jj in range(B):
                j = B * block + jj
                factor = jnp.broadcast_to(x[j : j + 1], (B, width)).astype(BF16)
                for part in range(block + 1):
                    at = START[block] + jj * n + B * part
                    pair_ref[at : at + B, :width] = low[B * part : B * (part + 1)] * factor
        first, begin, end = B * group[0], START[group[0]], START[group[-1] + 1]
        some = jnp.dot(coef[first:, begin:end], pair_ref[begin:end, :width], preferred_element_type=F32)
        gain = some if gain is None else jnp.concatenate([gain[:first], gain[first:] + some], axis=0)
    rate = jnp.dot(beta[...], low, preferred_element_type=F32)
    change = gain - x * rate
    return [change[:, CELLS * p : CELLS * (p + 1)] for p in range(len(planes))]


def moved(before, here, after, speed_before, speed_here):
    out = jnp.maximum(speed_here, 0.0) * here + jnp.minimum(speed_here, 0.0) * after
    came = jnp.maximum(speed_before, 0.0) * before + jnp.minimum(speed_before, 0.0) * here
    return here - (out - came)


def inner_faces(core, chip_ref, speed_ref):
    sign = (1 - 2 * core).astype(F32)
    for p in range(6):
        speed_ref[p : p + 1] = chip_ref[p, K : K + 1] + chip_ref[p, K + 1 : K + 2] * (1.0 / 2048.0)
    return [sign * speed_ref[pl.ds(4 * core + (1 - 2 * core) * f, 1)] for f in range(5)]


def inner(core, chip_ref, beta_ref, coef_ref, found, pair_ref, speed_ref):
    react1_ref, state1_ref, react2_ref, state2_ref, react3_ref = found
    faces = inner_faces(core, chip_ref, speed_ref)
    planes = [chip_ref[5 * core + (1 - 2 * core) * p, :K] for p in range(6)]
    changes = reaction(planes, beta_ref, coef_ref, pair_ref)
    react1_ref[0], react1_ref[1] = changes[0], changes[5]
    planes = [moved(*planes[p - 1 : p + 2], faces[p - 1], faces[p]) + changes[p] for p in range(1, 5)]
    for p in range(4):
        state1_ref[p] = planes[p]
    changes = reaction(planes, beta_ref, coef_ref, pair_ref)
    react2_ref[0], react2_ref[1] = changes[0], changes[3]
    planes = [moved(*planes[p - 1 : p + 2], faces[p], faces[p + 1]) + changes[p] for p in range(1, 3)]
    changes = reaction(planes, beta_ref, coef_ref, pair_ref)
    for p in range(2):
        state2_ref[p] = planes[p]
        react3_ref[p] = changes[p]


def before_kernel(place_ref, chip_ref, beta_ref, coef_ref, *refs):
    @pl.when(place_ref[1] == 0)
    def _():
        inner(place_ref[0], chip_ref, beta_ref, coef_ref, refs[:5], refs[5], refs[6])


def outer_kernel(place_ref, chip_ref, beta_ref, coef_ref, far_ref, near_ref, *refs):
    out_ref, found = refs[5], refs[6:11]
    pair_ref, speed_ref, state_ref, change_ref = refs[11:]
    react1_ref, state1_ref, react2_ref, state2_ref, react3_ref = found
    core = place_ref[0]
    step = 1 - 2 * core
    sign = step.astype(F32)

    @pl.when(place_ref[1] == 1)
    def _():
        inner(core, chip_ref, beta_ref, coef_ref, found, pair_ref, speed_ref)

    def speed(ref, p):
        return ref[p, K : K + 1] + ref[p, K + 1 : K + 2] * (1.0 / 2048.0)

    for p in range(4):
        speed_ref[p : p + 1] = speed(far_ref, 3 * core + step * p)
        state_ref[0, p] = far_ref[3 * core + step * p, :K]
    for p in range(6):
        speed_ref[4 + p : 5 + p] = speed(chip_ref, 5 * core + step * p)
        state_ref[0, 4 + p] = chip_ref[5 * core + step * p, :K]
    speed_ref[10:11] = near_ref[K : K + 1] + near_ref[K + 1 : K + 2] * (1.0 / 2048.0)
    state_ref[0, 10] = near_ref[:K]

    known_changes = [
        {4: (react1_ref, 0), 9: (react1_ref, 1)},
        {5: (react2_ref, 0), 8: (react2_ref, 1)},
        {6: (react3_ref, 0), 7: (react3_ref, 1)},
        {},
    ]
    known_states = [{5 + p: (state1_ref, p) for p in range(4)}, {6 + p: (state2_ref, p) for p in range(2)}, {}, {}]

    def transport(t):
        now, later = t % 2, (t + 1) % 2
        faces = [sign * speed_ref[pl.ds(core + f, 1)] for f in range(10)]
        change = {t + 1 + p: (change_ref, p) for p in range(3)} | known_changes[t]
        for w in range(t + 1, 10 - t):
            if w in known_states[t]:
                ref, at = known_states[t][w]
                state_ref[later, w] = ref[at]
            else:
                ref, at = change[w]
                near = [state_ref[now, v] for v in (w - 1, w, w + 1)]
                state_ref[later, w] = moved(*near, faces[w - 1], faces[w]) + ref[at]

    def advance(t, _):
        half = lax.rem(t, 2)
        planes = [state_ref[half, t + 1 + p] for p in range(3)]
        for p, change in enumerate(reaction(planes, beta_ref, coef_ref, pair_ref)):
            change_ref[p] = change
        for at in range(STEPS):
            pl.when(t == at)(lambda at=at: transport(at))
        return 0

    lax.fori_loop(0, STEPS, advance, 0)
    for p in range(3):
        value = state_ref[STEPS % 2, 4 + p] * (1.0 / 512.0)
        for d in range(16):
            out_ref[d, 2 * core + step * p] = value[8 * d : 8 * d + 8]


def scratch(planes, rows):
    return [pltpu.VMEM((PAIRS, planes * CELLS), BF16)] + [pltpu.VMEM((r, CELLS), F32) for r in rows]


def cost(planes):
    return pl.CostEstimate(flops=2 * K * 9216 * CELLS * planes, bytes_accessed=3000000, transcendentals=0)


def on_device(density, velocity, kernel, split, target):
    core = lax.axis_index("core").astype(jnp.int32)
    beta, coef = prepare(kernel, split, target)
    blocks = density.reshape(3, 8, 16, CELLS).astype(F16)
    blocks = lax.all_to_all(blocks, SECT, split_axis=2, concat_axis=2, tiled=True)
    speed = lax.dynamic_slice_in_dim(velocity, lax.axis_index(SECT) * CELLS, CELLS, 1)
    high = speed.astype(F16)
    rest = ((speed - high.astype(F32)) * 2048.0).astype(F16)
    own = blocks.transpose(0, 2, 1, 3).reshape(3, K, CELLS)
    own = jnp.concatenate([own, high[:, None], rest[:, None], jnp.zeros((3, 6, CELLS), F16)], axis=1)
    chip = lax.all_gather(own, "core", axis=0, tiled=True)
    place = jnp.stack([core, jnp.where(lax.axis_index("chip") % 4 < 2, 0, 1).astype(jnp.int32)])
    wide = chip.astype(F32)
    shapes = [jax.ShapeDtypeStruct((n, K, CELLS), F32) for n in (2, 4, 2, 2, 2)]
    found = pl.pallas_call(
        before_kernel,
        out_shape=shapes,
        in_specs=[SMEM] + [VMEM] * 3,
        out_specs=[VMEM] * 5,
        scratch_shapes=scratch(6, (8,)),
        compiler_params=params(24),
        cost_estimate=cost(12),
        name="before",
    )(place, wide, beta, coef)
    edge = lax.dynamic_slice_in_dim(chip, 2 * core, 4, 0)
    edge, found = lax.optimization_barrier((edge, found))
    neighbours = [[s, (s + 1) % 32] for s in range(1, 32, 2)]
    far = lax.all_gather(edge, SPACE, axis=0, axis_index_groups=neighbours)
    far = lax.dynamic_index_in_dim(far, core, 0, keepdims=False)
    near = lax.all_gather(lax.dynamic_index_in_dim(far, 3 * (1 - core), 0, keepdims=False), "core", axis=0)
    near = lax.dynamic_index_in_dim(near, 1 - core, 0, keepdims=False)
    blocks, *_ = pl.pallas_call(
        outer_kernel,
        out_shape=[jax.ShapeDtypeStruct((16, 3, 8, CELLS), F32), *shapes],
        in_specs=[SMEM] + [VMEM] * 10,
        out_specs=[VMEM] * 6,
        scratch_shapes=scratch(6, (16,)) + [pltpu.VMEM((2, 11, K, CELLS), F32), pltpu.VMEM((3, K, CELLS), F32)],
        input_output_aliases={6 + n: 1 + n for n in range(5)},
        compiler_params=params(32),
        cost_estimate=cost(12),
        name="outer",
    )(place, wide, beta, coef, far.astype(F32), near.astype(F32), *found)
    blocks = lax.all_to_all(blocks.astype(F16), SECT, split_axis=0, concat_axis=0, tiled=True)
    return blocks.transpose(1, 2, 0, 3).reshape(density.shape).astype(F32) * 512.0


def solution(mesh):
    torus = Mesh(mesh.devices.reshape(16, 2, 2, 8), ("chip", "core", "zl", "y"))
    return jax.shard_map(
        on_device,
        mesh=torus,
        in_specs=(P(SPACE, SECT, None), P(SPACE, None), P(), P(), P()),
        out_specs=P(SPACE, SECT, None),
        check_vma=False,
    )
```

```python
import jax
import jax.numpy as jnp
from jax import lax
from jax.experimental import pallas as pl
from jax.experimental.pallas import tpu as pltpu
from jax.sharding import Mesh
from jax.sharding import PartitionSpec as P

K = 128
CELLS = 128
BLOCKS = 8
B = 16
START = [K * b * (b + 1) for b in range(BLOCKS + 1)]
PAIRS = START[BLOCKS]
SECT = ("zl", "y")
SPACE = ("chip", "core")
STEPS = 4
VMEM = pl.BlockSpec(memory_space=pltpu.VMEM)
SMEM = pl.BlockSpec(memory_space=pltpu.SMEM)
F16 = jnp.float16
F32 = jnp.float32
BF16 = jnp.bfloat16


def params(mib):
    return pltpu.CompilerParams(vmem_limit_bytes=mib * 1024 * 1024)


def prepare_kernel(table_ref, beta_ref, coef_ref):
    kernel, split = table_ref[:K], table_ref[K : 2 * K]
    beta = 0.5 * (kernel + kernel.T)
    weight = 0.5 * (split + split.T)
    beta_ref[...] = beta.astype(BF16)
    rows = lax.broadcasted_iota(jnp.int32, (K, K), 0)
    cols = lax.broadcasted_iota(jnp.int32, (K, K), 1)
    count = jnp.where(cols < rows, 2.0, jnp.where(cols == rows, 1.0, 0.0))
    low = 0.5 * beta * weight * count
    high = 0.5 * beta * (1.0 - weight) * count
    target = jnp.where(cols <= rows, table_ref[2 * K :], 0.0).astype(jnp.int32)
    for block in range(BLOCKS):
        n = B * (block + 1)
        tiles = n * B // K
        parts = [[None] * tiles for _ in range(3)]
        for jj in range(B):
            j = B * block + jj
            for which, array in enumerate((low, high, target)):
                row = array[j : j + 1]
                offset = jj * n
                first, shift = offset // K, offset % K
                if shift:
                    row = pltpu.roll(row, shift, 1)
                lane = cols[:1]
                pieces = [(first, row)]
                if shift + n > K:
                    zero = jnp.zeros_like(row)
                    pieces = [(first, jnp.where(lane >= shift, row, zero)), (first + 1, jnp.where(lane < shift, row, zero))]
                for tile, piece in pieces:
                    had = parts[which][tile]
                    parts[which][tile] = piece if had is None else had + piece
        top = K - B * block
        ks = lax.broadcasted_iota(jnp.int32, (top, K), 0) + B * block
        for tile in range(tiles):
            a, b, t = (parts[which][tile] for which in range(3))
            value = jnp.where(ks == t, a, jnp.where(ks == t + 1, b, 0.0))
            at = START[block] + tile * K
            coef_ref[K - top :, at : at + K] = value.astype(BF16)
            if block:
                coef_ref[: K - top, at : at + K] = jnp.zeros((K - top, K), BF16)


def prepare(kernel, split, target):
    shapes = [jax.ShapeDtypeStruct((K, K), BF16), jax.ShapeDtypeStruct((K, PAIRS), BF16)]
    return pl.pallas_call(
        prepare_kernel,
        out_shape=shapes,
        in_specs=[VMEM],
        out_specs=[VMEM] * 2,
        compiler_params=params(16),
        name="prepare",
    )(jnp.concatenate([kernel, split, target.astype(F32)]))


def reaction(planes, beta, coef, pair_ref):
    x = jnp.concatenate(planes, axis=1) if len(planes) > 1 else planes[0]
    width = x.shape[1]
    low = x.astype(BF16)
    gain = None
    for group in [range(BLOCKS)] if len(planes) > 3 else [[block] for block in range(BLOCKS)]:
        for block in group:
            n = B * (block + 1)
            for jj in range(B):
                j = B * block + jj
                factor = jnp.broadcast_to(x[j : j + 1], (B, width)).astype(BF16)
                for part in range(block + 1):
                    at = START[block] + jj * n + B * part
                    pair_ref[at : at + B, :width] = low[B * part : B * (part + 1)] * factor
        first, begin, end = B * group[0], START[group[0]], START[group[-1] + 1]
        some = jnp.dot(coef[first:, begin:end], pair_ref[begin:end, :width], preferred_element_type=F32)
        gain = some if gain is None else jnp.concatenate([gain[:first], gain[first:] + some], axis=0)
    rate = jnp.dot(beta[...], low, preferred_element_type=F32)
    change = gain - x * rate
    return [change[:, CELLS * p : CELLS * (p + 1)] for p in range(len(planes))]


def moved(before, here, after, speed_before, speed_here):
    out = jnp.maximum(speed_here, 0.0) * here + jnp.minimum(speed_here, 0.0) * after
    came = jnp.maximum(speed_before, 0.0) * before + jnp.minimum(speed_before, 0.0) * here
    return here - (out - came)


def inner_faces(core, chip_ref, speed_ref):
    sign = (1 - 2 * core).astype(F32)
    for p in range(6):
        speed_ref[p : p + 1] = chip_ref[p, K : K + 1] + chip_ref[p, K + 1 : K + 2] * (1.0 / 2048.0)
    return [sign * speed_ref[pl.ds(4 * core + (1 - 2 * core) * f, 1)] for f in range(5)]


def inner(core, chip_ref, beta_ref, coef_ref, found, pair_ref, speed_ref):
    react1_ref, state1_ref, react2_ref, state2_ref, react3_ref = found
    faces = inner_faces(core, chip_ref, speed_ref)
    planes = [chip_ref[5 * core + (1 - 2 * core) * p, :K] for p in range(6)]
    changes = reaction(planes, beta_ref, coef_ref, pair_ref)
    react1_ref[0], react1_ref[1] = changes[0], changes[5]
    planes = [moved(*planes[p - 1 : p + 2], faces[p - 1], faces[p]) + changes[p] for p in range(1, 5)]
    for p in range(4):
        state1_ref[p] = planes[p]
    changes = reaction(planes, beta_ref, coef_ref, pair_ref)
    react2_ref[0], react2_ref[1] = changes[0], changes[3]
    planes = [moved(*planes[p - 1 : p + 2], faces[p], faces[p + 1]) + changes[p] for p in range(1, 3)]
    changes = reaction(planes, beta_ref, coef_ref, pair_ref)
    for p in range(2):
        state2_ref[p] = planes[p]
        react3_ref[p] = changes[p]


def before_kernel(place_ref, chip_ref, beta_ref, coef_ref, *refs):
    @pl.when(place_ref[1] == 0)
    def _():
        inner(place_ref[0], chip_ref, beta_ref, coef_ref, refs[:5], refs[5], refs[6])


def outer_kernel(place_ref, chip_ref, beta_ref, coef_ref, far_ref, near_ref, *refs):
    out_ref, found = refs[5], refs[6:11]
    pair_ref, speed_ref, state_ref, change_ref = refs[11:]
    react1_ref, state1_ref, react2_ref, state2_ref, react3_ref = found
    core = place_ref[0]
    step = 1 - 2 * core
    sign = step.astype(F32)

    @pl.when(place_ref[1] == 1)
    def _():
        inner(core, chip_ref, beta_ref, coef_ref, found, pair_ref, speed_ref)

    def speed(ref, p):
        return ref[p, K : K + 1] + ref[p, K + 1 : K + 2] * (1.0 / 2048.0)

    for p in range(4):
        speed_ref[p : p + 1] = speed(far_ref, 3 * core + step * p)
        state_ref[0, p] = far_ref[3 * core + step * p, :K]
    for p in range(6):
        speed_ref[4 + p : 5 + p] = speed(chip_ref, 5 * core + step * p)
        state_ref[0, 4 + p] = chip_ref[5 * core + step * p, :K]
    speed_ref[10:11] = near_ref[K : K + 1] + near_ref[K + 1 : K + 2] * (1.0 / 2048.0)
    state_ref[0, 10] = near_ref[:K]

    known_changes = [
        {4: (react1_ref, 0), 9: (react1_ref, 1)},
        {5: (react2_ref, 0), 8: (react2_ref, 1)},
        {6: (react3_ref, 0), 7: (react3_ref, 1)},
        {},
    ]
    known_states = [{5 + p: (state1_ref, p) for p in range(4)}, {6 + p: (state2_ref, p) for p in range(2)}, {}, {}]

    def transport(t):
        now, later = t % 2, (t + 1) % 2
        faces = [sign * speed_ref[pl.ds(core + f, 1)] for f in range(10)]
        change = {t + 1 + p: (change_ref, p) for p in range(3)} | known_changes[t]
        for w in range(t + 1, 10 - t):
            if w in known_states[t]:
                ref, at = known_states[t][w]
                state_ref[later, w] = ref[at]
            else:
                ref, at = change[w]
                near = [state_ref[now, v] for v in (w - 1, w, w + 1)]
                state_ref[later, w] = moved(*near, faces[w - 1], faces[w]) + ref[at]

    def advance(t, _):
        half = lax.rem(t, 2)
        planes = [state_ref[half, t + 1 + p] for p in range(3)]
        for p, change in enumerate(reaction(planes, beta_ref, coef_ref, pair_ref)):
            change_ref[p] = change
        for at in range(STEPS):
            pl.when(t == at)(lambda at=at: transport(at))
        return 0

    lax.fori_loop(0, STEPS, advance, 0)
    for p in range(3):
        value = state_ref[STEPS % 2, 4 + p] * (1.0 / 512.0)
        for d in range(16):
            out_ref[d, 2 * core + step * p] = value[8 * d : 8 * d + 8]


def scratch(planes, rows):
    return [pltpu.VMEM((PAIRS, planes * CELLS), BF16)] + [pltpu.VMEM((r, CELLS), F32) for r in rows]


def cost(planes):
    return pl.CostEstimate(flops=2 * K * 9216 * CELLS * planes, bytes_accessed=3000000, transcendentals=0)


def on_device(density, velocity, kernel, split, target):
    core = lax.axis_index("core").astype(jnp.int32)
    beta, coef = prepare(kernel, split, target)
    blocks = density.reshape(3, 8, 16, CELLS).astype(F16)
    blocks = lax.all_to_all(blocks, SECT, split_axis=2, concat_axis=2, tiled=True)
    speed = lax.dynamic_slice_in_dim(velocity, lax.axis_index(SECT) * CELLS, CELLS, 1)
    high = speed.astype(F16)
    rest = ((speed - high.astype(F32)) * 2048.0).astype(F16)
    own = blocks.transpose(0, 2, 1, 3).reshape(3, K, CELLS)
    own = jnp.concatenate([own, high[:, None], rest[:, None], jnp.zeros((3, 6, CELLS), F16)], axis=1)
    chip = lax.all_gather(own, "core", axis=0, tiled=True)
    place = jnp.stack([core, jnp.where(lax.axis_index("chip") % 4 < 2, 0, 1).astype(jnp.int32)])
    wide = chip.astype(F32)
    shapes = [jax.ShapeDtypeStruct((n, K, CELLS), F32) for n in (2, 4, 2, 2, 2)]
    found = pl.pallas_call(
        before_kernel,
        out_shape=shapes,
        in_specs=[SMEM] + [VMEM] * 3,
        out_specs=[VMEM] * 5,
        scratch_shapes=scratch(6, (8,)),
        compiler_params=params(24),
        cost_estimate=cost(12),
        name="before",
    )(place, wide, beta, coef)
    edge = lax.dynamic_slice_in_dim(chip, 2 * core, 4, 0)
    edge = jnp.concatenate([edge[:, :K].reshape(4 * K, CELLS), edge[:, K : K + 2].reshape(8, CELLS)])
    edge, found = lax.optimization_barrier((edge, found))
    neighbours = [[s, (s + 1) % 32] for s in range(1, 32, 2)]
    far = lax.all_gather(edge, SPACE, axis=0, axis_index_groups=neighbours)
    far = lax.dynamic_index_in_dim(far, core, 0, keepdims=False)
    far = jnp.concatenate([far[: 4 * K].reshape(4, K, CELLS), far[4 * K :].reshape(4, 2, CELLS)], axis=1)
    near = lax.all_gather(lax.dynamic_index_in_dim(far, 3 * (1 - core), 0, keepdims=False), "core", axis=0)
    near = lax.dynamic_index_in_dim(near, 1 - core, 0, keepdims=False)
    blocks, *_ = pl.pallas_call(
        outer_kernel,
        out_shape=[jax.ShapeDtypeStruct((16, 3, 8, CELLS), F32), *shapes],
        in_specs=[SMEM] + [VMEM] * 10,
        out_specs=[VMEM] * 6,
        scratch_shapes=scratch(6, (16,)) + [pltpu.VMEM((2, 11, K, CELLS), F32), pltpu.VMEM((3, K, CELLS), F32)],
        input_output_aliases={6 + n: 1 + n for n in range(5)},
        compiler_params=params(32),
        cost_estimate=cost(12),
        name="outer",
    )(place, wide, beta, coef, far.astype(F32), near.astype(F32), *found)
    blocks = lax.all_to_all(blocks.astype(F16), SECT, split_axis=0, concat_axis=0, tiled=True)
    return blocks.transpose(1, 2, 0, 3).reshape(density.shape).astype(F32) * 512.0


def solution(mesh):
    torus = Mesh(mesh.devices.reshape(16, 2, 2, 8), ("chip", "core", "zl", "y"))
    return jax.shard_map(
        on_device,
        mesh=torus,
        in_specs=(P(SPACE, SECT, None), P(SPACE, None), P(), P(), P()),
        out_specs=P(SPACE, SECT, None),
        check_vma=False,
    )
```

```python
import jax
import jax.numpy as jnp
from jax import lax
from jax.experimental import pallas as pl
from jax.experimental.pallas import tpu as pltpu
from jax.sharding import Mesh
from jax.sharding import PartitionSpec as P

K = 128
CELLS = 128
BLOCKS = 8
B = 16
START = [K * b * (b + 1) for b in range(BLOCKS + 1)]
PAIRS = START[BLOCKS]
SECT = ("zl", "y")
SPACE = ("chip", "core")
STEPS = 4
VMEM = pl.BlockSpec(memory_space=pltpu.VMEM)
SMEM = pl.BlockSpec(memory_space=pltpu.SMEM)
F16 = jnp.float16
F32 = jnp.float32
BF16 = jnp.bfloat16


def params(mib):
    return pltpu.CompilerParams(vmem_limit_bytes=mib * 1024 * 1024)


def prepare_kernel(table_ref, beta_ref, coef_ref):
    kernel, split = table_ref[:K], table_ref[K : 2 * K]
    beta = 0.5 * (kernel + kernel.T)
    weight = 0.5 * (split + split.T)
    beta_ref[...] = beta.astype(BF16)
    rows = lax.broadcasted_iota(jnp.int32, (K, K), 0)
    cols = lax.broadcasted_iota(jnp.int32, (K, K), 1)
    count = jnp.where(cols < rows, 2.0, jnp.where(cols == rows, 1.0, 0.0))
    low = 0.5 * beta * weight * count
    high = 0.5 * beta * (1.0 - weight) * count
    target = jnp.where(cols <= rows, table_ref[2 * K :], 0.0).astype(jnp.int32)
    for block in range(BLOCKS):
        n = B * (block + 1)
        tiles = n * B // K
        parts = [[None] * tiles for _ in range(3)]
        for jj in range(B):
            j = B * block + jj
            for which, array in enumerate((low, high, target)):
                row = array[j : j + 1]
                offset = jj * n
                first, shift = offset // K, offset % K
                if shift:
                    row = pltpu.roll(row, shift, 1)
                lane = cols[:1]
                pieces = [(first, row)]
                if shift + n > K:
                    zero = jnp.zeros_like(row)
                    pieces = [(first, jnp.where(lane >= shift, row, zero)), (first + 1, jnp.where(lane < shift, row, zero))]
                for tile, piece in pieces:
                    had = parts[which][tile]
                    parts[which][tile] = piece if had is None else had + piece
        top = K - B * block
        ks = lax.broadcasted_iota(jnp.int32, (top, K), 0) + B * block
        for tile in range(tiles):
            a, b, t = (parts[which][tile] for which in range(3))
            value = jnp.where(ks == t, a, jnp.where(ks == t + 1, b, 0.0))
            at = START[block] + tile * K
            coef_ref[K - top :, at : at + K] = value.astype(BF16)
            if block:
                coef_ref[: K - top, at : at + K] = jnp.zeros((K - top, K), BF16)


def prepare(kernel, split, target):
    shapes = [jax.ShapeDtypeStruct((K, K), BF16), jax.ShapeDtypeStruct((K, PAIRS), BF16)]
    return pl.pallas_call(
        prepare_kernel,
        out_shape=shapes,
        in_specs=[VMEM],
        out_specs=[VMEM] * 2,
        compiler_params=params(16),
        name="prepare",
    )(jnp.concatenate([kernel, split, target.astype(F32)]))


def reaction(planes, beta, coef, pair_ref):
    x = jnp.concatenate(planes, axis=1) if len(planes) > 1 else planes[0]
    width = x.shape[1]
    low = x.astype(BF16)
    gain = None
    for group in [range(BLOCKS)] if len(planes) > 3 else [[block] for block in range(BLOCKS)]:
        for block in group:
            n = B * (block + 1)
            for jj in range(B):
                j = B * block + jj
                factor = jnp.broadcast_to(x[j : j + 1], (B, width)).astype(BF16)
                for part in range(block + 1):
                    at = START[block] + jj * n + B * part
                    pair_ref[at : at + B, :width] = low[B * part : B * (part + 1)] * factor
        first, begin, end = B * group[0], START[group[0]], START[group[-1] + 1]
        some = jnp.dot(coef[first:, begin:end], pair_ref[begin:end, :width], preferred_element_type=F32)
        gain = some if gain is None else jnp.concatenate([gain[:first], gain[first:] + some], axis=0)
    rate = jnp.dot(beta[...], low, preferred_element_type=F32)
    change = gain - x * rate
    return [change[:, CELLS * p : CELLS * (p + 1)] for p in range(len(planes))]


def moved(before, here, after, speed_before, speed_here):
    out = jnp.maximum(speed_here, 0.0) * here + jnp.minimum(speed_here, 0.0) * after
    came = jnp.maximum(speed_before, 0.0) * before + jnp.minimum(speed_before, 0.0) * here
    return here - (out - came)


def inner_faces(core, chip_ref, speed_ref):
    sign = (1 - 2 * core).astype(F32)
    for p in range(6):
        speed_ref[p : p + 1] = chip_ref[p, K : K + 1] + chip_ref[p, K + 1 : K + 2] * (1.0 / 2048.0)
    return [sign * speed_ref[pl.ds(4 * core + (1 - 2 * core) * f, 1)] for f in range(5)]


def inner(core, chip_ref, beta_ref, coef_ref, found, pair_ref, speed_ref):
    react1_ref, state1_ref, react2_ref, state2_ref, react3_ref = found
    faces = inner_faces(core, chip_ref, speed_ref)
    planes = [chip_ref[5 * core + (1 - 2 * core) * p, :K] for p in range(6)]
    changes = reaction(planes, beta_ref, coef_ref, pair_ref)
    react1_ref[0], react1_ref[1] = changes[0], changes[5]
    planes = [moved(*planes[p - 1 : p + 2], faces[p - 1], faces[p]) + changes[p] for p in range(1, 5)]
    for p in range(4):
        state1_ref[p] = planes[p]
    changes = reaction(planes, beta_ref, coef_ref, pair_ref)
    react2_ref[0], react2_ref[1] = changes[0], changes[3]
    planes = [moved(*planes[p - 1 : p + 2], faces[p], faces[p + 1]) + changes[p] for p in range(1, 3)]
    changes = reaction(planes, beta_ref, coef_ref, pair_ref)
    for p in range(2):
        state2_ref[p] = planes[p]
        react3_ref[p] = changes[p]


def before_kernel(place_ref, chip_ref, beta_ref, coef_ref, *refs):
    @pl.when(place_ref[1] == 0)
    def _():
        inner(place_ref[0], chip_ref, beta_ref, coef_ref, refs[:5], refs[5], refs[6])


def outer_kernel(place_ref, chip_ref, beta_ref, coef_ref, far_ref, near_ref, *refs):
    out_ref, found = refs[5], refs[6:11]
    pair_ref, speed_ref, state_ref, change_ref = refs[11:]
    react1_ref, state1_ref, react2_ref, state2_ref, react3_ref = found
    core = place_ref[0]
    step = 1 - 2 * core
    sign = step.astype(F32)

    @pl.when(place_ref[1] == 1)
    def _():
        inner(core, chip_ref, beta_ref, coef_ref, found, pair_ref, speed_ref)

    def speed(ref, p):
        return ref[p, K : K + 1] + ref[p, K + 1 : K + 2] * (1.0 / 2048.0)

    for p in range(4):
        speed_ref[p : p + 1] = speed(far_ref, 3 * core + step * p)
        state_ref[0, p] = far_ref[3 * core + step * p, :K]
    for p in range(6):
        speed_ref[4 + p : 5 + p] = speed(chip_ref, 5 * core + step * p)
        state_ref[0, 4 + p] = chip_ref[5 * core + step * p, :K]
    speed_ref[10:11] = near_ref[K : K + 1] + near_ref[K + 1 : K + 2] * (1.0 / 2048.0)
    state_ref[0, 10] = near_ref[:K]

    known_changes = [
        {4: (react1_ref, 0), 9: (react1_ref, 1)},
        {5: (react2_ref, 0), 8: (react2_ref, 1)},
        {6: (react3_ref, 0), 7: (react3_ref, 1)},
        {},
    ]
    known_states = [{5 + p: (state1_ref, p) for p in range(4)}, {6 + p: (state2_ref, p) for p in range(2)}, {}, {}]

    def transport(t):
        now, later = t % 2, (t + 1) % 2
        faces = [sign * speed_ref[pl.ds(core + f, 1)] for f in range(10)]
        change = {t + 1 + p: (change_ref, p) for p in range(3)} | known_changes[t]
        for w in range(t + 1, 10 - t):
            if w in known_states[t]:
                ref, at = known_states[t][w]
                state_ref[later, w] = ref[at]
            else:
                ref, at = change[w]
                near = [state_ref[now, v] for v in (w - 1, w, w + 1)]
                state_ref[later, w] = moved(*near, faces[w - 1], faces[w]) + ref[at]

    def advance(t, _):
        half = lax.rem(t, 2)
        planes = [state_ref[half, t + 1 + p] for p in range(3)]
        for p, change in enumerate(reaction(planes, beta_ref, coef_ref, pair_ref)):
            change_ref[p] = change
        for at in range(STEPS):
            pl.when(t == at)(lambda at=at: transport(at))
        return 0

    lax.fori_loop(0, STEPS, advance, 0)
    for p in range(3):
        value = state_ref[STEPS % 2, 4 + p] * (1.0 / 512.0)
        for d in range(16):
            out_ref[d, 2 * core + step * p] = value[8 * d : 8 * d + 8]


def scratch(planes, rows):
    return [pltpu.VMEM((PAIRS, planes * CELLS), BF16)] + [pltpu.VMEM((r, CELLS), F32) for r in rows]


def cost(planes):
    return pl.CostEstimate(flops=2 * K * 9216 * CELLS * planes, bytes_accessed=3000000, transcendentals=0)


def on_device(density, velocity, kernel, split, target):
    core = lax.axis_index("core").astype(jnp.int32)
    beta, coef = prepare(kernel, split, target)
    blocks = density.reshape(3, 8, 16, CELLS).astype(F16)
    blocks = lax.all_to_all(blocks, SECT, split_axis=2, concat_axis=2, tiled=True)
    speed = lax.dynamic_slice_in_dim(velocity, lax.axis_index(SECT) * CELLS, CELLS, 1)
    high = speed.astype(F16)
    rest = ((speed - high.astype(F32)) * 2048.0).astype(F16)
    own = blocks.transpose(0, 2, 1, 3).reshape(3, K, CELLS)
    own = jnp.concatenate([own, high[:, None], rest[:, None], jnp.zeros((3, 6, CELLS), F16)], axis=1)
    chip = lax.all_gather(own, "core", axis=0, tiled=True)
    place = jnp.stack([core, jnp.where(lax.axis_index("chip") % 4 < 1, 0, 1).astype(jnp.int32)])
    wide = chip.astype(F32)
    shapes = [jax.ShapeDtypeStruct((n, K, CELLS), F32) for n in (2, 4, 2, 2, 2)]
    found = pl.pallas_call(
        before_kernel,
        out_shape=shapes,
        in_specs=[SMEM] + [VMEM] * 3,
        out_specs=[VMEM] * 5,
        scratch_shapes=scratch(6, (8,)),
        compiler_params=params(24),
        cost_estimate=cost(12),
        name="before",
    )(place, wide, beta, coef)
    edge = lax.dynamic_slice_in_dim(chip, 2 * core, 4, 0)
    edge, found = lax.optimization_barrier((edge, found))
    neighbours = [[s, (s + 1) % 32] for s in range(1, 32, 2)]
    far = lax.all_gather(edge, SPACE, axis=0, axis_index_groups=neighbours)
    far = lax.dynamic_index_in_dim(far, core, 0, keepdims=False)
    near = lax.all_gather(lax.dynamic_index_in_dim(far, 3 * (1 - core), 0, keepdims=False), "core", axis=0)
    near = lax.dynamic_index_in_dim(near, 1 - core, 0, keepdims=False)
    blocks, *_ = pl.pallas_call(
        outer_kernel,
        out_shape=[jax.ShapeDtypeStruct((16, 3, 8, CELLS), F32), *shapes],
        in_specs=[SMEM] + [VMEM] * 10,
        out_specs=[VMEM] * 6,
        scratch_shapes=scratch(6, (16,)) + [pltpu.VMEM((2, 11, K, CELLS), F32), pltpu.VMEM((3, K, CELLS), F32)],
        input_output_aliases={6 + n: 1 + n for n in range(5)},
        compiler_params=params(32),
        cost_estimate=cost(12),
        name="outer",
    )(place, wide, beta, coef, far.astype(F32), near.astype(F32), *found)
    blocks = lax.all_to_all(blocks.astype(F16), SECT, split_axis=0, concat_axis=0, tiled=True)
    return blocks.transpose(1, 2, 0, 3).reshape(density.shape).astype(F32) * 512.0


def solution(mesh):
    torus = Mesh(mesh.devices.reshape(16, 2, 2, 8), ("chip", "core", "zl", "y"))
    return jax.shard_map(
        on_device,
        mesh=torus,
        in_specs=(P(SPACE, SECT, None), P(SPACE, None), P(), P(), P()),
        out_specs=P(SPACE, SECT, None),
        check_vma=False,
    )
```
